256 devices in a mesh: dp: 32 (over y, x, core), mp: 8 (over z).
Axes of the slice: x: 4, y: 4, z: 8, core: 2. Of those that a mesh axis runs over, the one named last changes fastest.
Arguments:
- hidden: bfloat16 [192, 128, 4096], P('dp'), may hold values from -6 to 6
- norm_gain: bfloat16 [4096], replicated, may hold values from 0.25 to 1.75
- w_query: bfloat16 [4096, 4096], P('dp', 'mp'), may hold values from -0.09375 to 0.09375
- w_kv: bfloat16 [4096, 2, 1024], P('dp', None, 'mp'), may hold values from -0.09375 to 0.09375
- w_out: bfloat16 [4096, 4096], P('mp', 'dp'), may hold values from -0.09375 to 0.09375
- w_head: float32 [4096], replicated, may hold values from -0.75 to 0.75
- parents: int32 [192, 16], replicated, may hold values from -1 to 191, as said below
- lengths: int32 [192], replicated, may hold values from 64 to 128, as said below
Outputs:
- layer_out: bfloat16 [192, 128, 4096], P('dp', None, 'mp')
- values: float32 [192], P('dp')
The draws below stay inside these ranges and needn't reach their ends.
Inputs may be any that keep to these rules, and one draw needn't show every extreme that they name: `parents`: row n lists the ancestors of node n, nearest first, then -1 for the levels it lacks; the list of a node is its parent followed by the parent's list. All 6 nodes held by one index of dp have the same list, and the nodes in a list are held by distinct indices of dp, none the node's own. Some node has 16 ancestors. `lengths`: the used token slots of a node segment are its first ones.
All inputs are finite; a program needn't handle non-finite values.
Results may differ from the reference program's by a relative error of at most 0.017.
Values may be sent and summed in bfloat16 or wider, within the bound.
A program may use at most 128 MiB of HBM per device.

```python
import jax
import jax.numpy as jnp
from jax import lax

D = 4096
HS = 128
HEADS = 32
KV_HEADS = 8
BLK = 128
SLOTS = 6
DEPTH = 16
BLOCKS = 192
N_MP = 8


def draw_parents(key, part):
    key = jax.random.fold_in(key, 11)
    devices = BLOCKS // SLOTS
    key_order, key_slot = jax.random.split(key, 2)
    order = jax.random.permutation(key_order, devices).astype(jnp.int32)
    slot_pick = jax.random.randint(key_slot, (devices,), 0, SLOTS).astype(jnp.int32)
    chain = jnp.full((devices, DEPTH), -1, jnp.int32)

    def advance(rank, chain):
        chosen = jnp.where(rank <= DEPTH, rank - 1, DEPTH - 1)
        block = order[chosen] * SLOTS + slot_pick[chosen]
        row = jnp.concatenate([block[None], chain[chosen][:DEPTH - 1]], 0)
        return chain.at[rank].set(row)
    chain = lax.fori_loop(1, devices, advance, chain)
    rank_of = jnp.argsort(order).astype(jnp.int32)
    rows = chain[rank_of]
    return jnp.repeat(rows, SLOTS, axis=0).astype(jnp.int32)


def draw_lengths(key, part):
    key = jax.random.fold_in(key, 23)
    key_len, key_spot = jax.random.split(key)
    counts = jax.random.randint(key_len, (BLOCKS,), BLK // 2, BLK + 1).astype(jnp.int32)
    spot = jax.random.randint(key_spot, (), 0, BLOCKS)
    return counts.at[spot].set(BLK).astype(jnp.int32)


def steps_of(stream_key, shape, cuts, smallest, top_value):
    factor_of = 1.0
    for dim, shards_of in cuts:
        steps = jax.random.uniform(jax.random.fold_in(jax.random.fold_in(stream_key, 6), dim), (shards_of,), jnp.float32, smallest / len(cuts), top_value / len(cuts))
        factor_of = factor_of * jnp.repeat(jnp.exp(steps), shape[dim] // shards_of).reshape((-1,) + (1,) * (len(shape) - 1 - dim))
    return factor_of


def centred(own_key, shape, scale, reach, pieces=(), kind=jnp.bfloat16):
    array = jax.random.normal(own_key, shape, jnp.float32) * scale
    if len(pieces) > 0:
        array = steps_of(own_key, shape, pieces, -0.22, 0.18) * array
    return jnp.clip(array, min=-reach, max=reach).astype(kind)


def setup_inputs(seed: int = 0) -> dict:
    key_list = jax.random.split(jax.random.key(seed), 9)
    return {
        "hidden": centred(key_list[0], (BLOCKS, BLK, D), 1.0, 6.0, ((0, 32),)),
        "norm_gain": jnp.clip(1.0 + 0.15 * jax.random.normal(key_list[1], (D,), jnp.float32), 0.25, 1.75).astype(jnp.bfloat16),
        "w_query": centred(key_list[2], (D, HEADS * HS), D ** -0.5, 0.09375, ((0, 32), (1, 8))),
        "w_kv": centred(key_list[3], (D, 2, KV_HEADS * HS), D ** -0.5, 0.09375, ((0, 32), (2, 8))),
        "w_out": centred(key_list[4], (HEADS * HS, D), (HEADS * HS) ** -0.5, 0.09375, ((0, 8), (1, 32))),
        "w_head": centred(key_list[5], (D,), 0.125, 0.75, (), jnp.float32),
        "parents": draw_parents(jax.random.fold_in(key_list[8], 71), 0),
        "lengths": draw_lengths(jax.random.fold_in(key_list[8], 71), 0),
    }


def unit_rows(rows):
    floats = rows.astype(jnp.float32)
    meansq = lax.optimization_barrier(jnp.mean(floats * floats, axis=-1, keepdims=True))
    return floats * lax.rsqrt(meansq + 1e-05)

def reference(hidden, norm_gain, w_query, w_kv, w_out, w_head, parents, lengths):
    width = HEADS * HS
    sharing = HEADS // KV_HEADS
    rows = hidden.reshape(BLOCKS * BLK, D)
    normed = (unit_rows(rows) * norm_gain.astype(jnp.float32)).astype(jnp.bfloat16)
    query = jnp.dot(normed, w_query, preferred_element_type=jnp.float32).astype(jnp.bfloat16)
    kv_proj = jnp.dot(normed, w_kv.reshape(D, 2 * KV_HEADS * HS), preferred_element_type=jnp.float32).astype(jnp.bfloat16)
    kv_proj = kv_proj.reshape(BLOCKS * BLK, 2, KV_HEADS * HS)
    query = query.reshape(BLOCKS, BLK, KV_HEADS, sharing, HS)
    keyed = kv_proj[:, 0].reshape(BLOCKS, BLK, KV_HEADS, HS)
    valued = kv_proj[:, 1].reshape(BLOCKS, BLK, KV_HEADS, HS)
    scale = 1.0 / HS ** 0.5
    token = jnp.arange(BLK, dtype=jnp.int32)

    def attend(node):
        chain = parents[node]
        safe = jnp.maximum(chain, 0)
        keys = jnp.concatenate([keyed[node][None], keyed[safe]], 0).reshape((1 + DEPTH) * BLK, KV_HEADS, HS)
        vals = jnp.concatenate([valued[node][None], valued[safe]], 0).reshape((1 + DEPTH) * BLK, KV_HEADS, HS)
        key_len = jnp.concatenate([lengths[node][None], jnp.where(chain >= 0, lengths[safe], 0)], 0)
        live = (token[None, :] < key_len[:, None]).reshape(-1)
        own = jnp.concatenate([jnp.ones((1, BLK), bool), jnp.zeros((DEPTH, BLK), bool)], 0).reshape(-1)
        kpos = jnp.tile(token, 1 + DEPTH)
        visible = live[None, :] & (~own[None, :] | (kpos[None, :] <= token[:, None]))
        scores = jnp.einsum('tkgd,ukd->kgtu', query[node].astype(jnp.float32), keys.astype(jnp.float32)) * scale
        weights = jnp.where(visible[None, None], jnp.exp(scores), 0.0)
        probs = (weights / lax.optimization_barrier(jnp.sum(weights, axis=-1, keepdims=True))).astype(jnp.bfloat16)
        out = jnp.einsum('kgtu,ukd->tkgd', probs.astype(jnp.float32), vals.astype(jnp.float32))
        return out.reshape(BLK, width).astype(jnp.bfloat16)
    attn = lax.map(attend, jnp.arange(BLOCKS, dtype=jnp.int32)).reshape(BLOCKS * BLK, width)
    group = width // N_MP
    total = jnp.zeros((BLOCKS * BLK, D), jnp.float32)
    for index in range(N_MP):
        partial_value = jnp.dot(attn[:, index * group:(index + 1) * group], w_out[index * group:(index + 1) * group], preferred_element_type=jnp.float32)
        total = total + partial_value.astype(jnp.bfloat16).astype(jnp.float32)
    layer_out = (rows.astype(jnp.float32) + total).astype(jnp.bfloat16)
    floats = layer_out.astype(jnp.float32)
    sumsq = lax.optimization_barrier(jnp.sum(floats * floats, axis=-1))
    product = lax.optimization_barrier(jnp.sum(floats * w_head[None, :], axis=-1))
    token_score = (product * lax.rsqrt(sumsq / D + 1e-05)).reshape(BLOCKS, BLK)
    used = token[None, :] < lengths[:, None]
    node_score = lax.optimization_barrier(jnp.sum(jnp.where(used, token_score, 0.0), axis=1)) / lengths.astype(jnp.float32)
    onehot = (parents[:, :, None] == jnp.arange(BLOCKS, dtype=jnp.int32)[None, None, :]).astype(jnp.float32)
    values = node_score + lax.optimization_barrier(jnp.sum(node_score[:, None, None] * onehot, axis=(0, 1)))
    return (layer_out.reshape(BLOCKS, BLK, D), values)
```

```python
import functools
import math

import jax
import jax.numpy as jnp
from jax import lax
from jax.experimental import pallas as pl
from jax.experimental.pallas import tpu as pltpu
from jax.sharding import PartitionSpec as P

HS = 128
V_SCALE = 2.0**-10
F32 = jnp.float32
BF16 = jnp.bfloat16
MESH = pl.DeviceIdType.MESH


def start_copy(src, dst, send_sem, recv_sem, device):
    pltpu.make_async_remote_copy(
        src_ref=src, dst_ref=dst, send_sem=send_sem, recv_sem=recv_sem,
        device_id=device, device_id_type=MESH,
    ).start()


def await_recv(ref, send_sem, recv_sem, device):
    pltpu.make_async_remote_copy(
        src_ref=ref, dst_ref=ref, send_sem=send_sem, recv_sem=recv_sem,
        device_id=device, device_id_type=MESH,
    ).wait_recv()


def await_send(ref, send_sem, recv_sem, device):
    pltpu.make_async_remote_copy(
        src_ref=ref, dst_ref=ref, send_sem=send_sem, recv_sem=recv_sem,
        device_id=device, device_id_type=MESH,
    ).wait_send()


class Gather:
    def __init__(self, part, whole, send_sem, sems, me, mp):
        self.part, self.whole = part, whole
        self.send_sem, self.sems = send_sem, sems
        self.mp = mp
        core = lax.rem(me, 2)
        x = lax.rem(lax.div(me, 2), 4)
        y = lax.div(me, 8)
        first = core == 0
        self.f0 = jnp.where(first, x, y)
        self.g0 = jnp.where(first, y, x)
        self.core = core
        self.fmul = jnp.where(first, 2, 8)
        self.gmul = jnp.where(first, 8, 2)
        self.me = me
        self.sibling = me + 1 - 2 * core
        self.steps = (0, 3, 1, 2)

    def index(self, f, g):
        f = lax.rem(self.f0 + f, 4)
        g = lax.rem(self.g0 + g, 4)
        return f * self.fmul + g * self.gmul + self.core

    def other_index(self, i, k):
        f = lax.rem(self.g0 + self.steps[i], 4)
        g = lax.rem(self.f0 + self.steps[k], 4)
        return f * self.gmul + g * self.fmul + 1 - self.core

    def send(self, block, half, sem, to):
        ref = self.part(block, half)
        start_copy(ref, ref, self.send_sem, self.sems.at[sem], (to, self.mp))

    def recv(self, block, half, sem):
        ref = self.part(block, half)
        await_recv(ref, self.send_sem, self.sems.at[sem], (self.sibling, self.mp))

    def spread(self, i):
        block = self.index(self.steps[i], 0)
        self.send(block, None, 4 + i, self.index(0, 1))
        self.send(block, None, 8 + i, self.index(0, 3))
        self.send(block, None, 20 + 4 * i, self.sibling)

    def begin(self):
        block = self.index(0, 0)
        self.send(block, None, 0, self.index(1, 0))
        self.send(block, None, 1, self.index(3, 0))
        self.spread(0)

    def first_ring(self):
        block = self.index(3, 0)
        self.recv(block, None, 0)
        self.send(block, 0, 2, self.index(1, 0))
        self.spread(1)
        block = self.index(1, 0)
        self.recv(block, None, 1)
        self.send(block, 1, 3, self.index(3, 0))
        self.spread(2)

    def first_ring_far(self):
        block = self.index(2, 0)
        self.recv(block, 0, 2)
        self.recv(block, 1, 3)
        self.spread(3)

    def second_ring(self, i):
        f = self.steps[i]
        block = self.index(f, 3)
        self.recv(block, None, 4 + i)
        self.send(block, 0, 12 + i, self.index(0, 1))
        self.send(block, None, 20 + 4 * i + 1, self.sibling)
        block = self.index(f, 1)
        self.recv(block, None, 8 + i)
        self.send(block, 1, 16 + i, self.index(0, 3))
        self.send(block, None, 20 + 4 * i + 2, self.sibling)

    def second_ring_far(self, i):
        block = self.index(self.steps[i], 2)
        self.recv(block, 0, 12 + i)
        self.recv(block, 1, 16 + i)
        self.send(block, None, 20 + 4 * i + 3, self.sibling)

    def from_sibling(self):
        for i in range(4):
            for k in range(4):
                self.recv(self.other_index(i, k), None, 20 + 4 * i + k)

    def events(self):
        return [
            self.first_ring,
            lambda: self.second_ring(0),
            self.first_ring_far,
            lambda: self.second_ring(1),
            lambda: (self.second_ring(2), self.second_ring_far(0)),
            lambda: (self.second_ring(3), self.second_ring_far(1)),
            lambda: (self.second_ring_far(2), self.second_ring_far(3)),
            self.from_sibling,
        ]

    def end(self):
        await_send(self.whole, self.send_sem, self.sems.at[0], (self.sibling, self.mp))


def kernel(
    n_dp, n_mp, slots, levels,
    hidden, gain, w_query, w_kv, w_out, w_head, wanted, src, anc_len, own_len, lens, hits,
    out, values,
    x, own_hidden, wq, wkv, wo, q, kv, kv_out, kv_in, keys, vals, near_v, near_w, far_w, attn,
    part, half_in, full_in, stat, stats, scores,
    local_sem, send_sem, kv_sem, q_sem, o_sem, a2a_sem, half_sem, full_sem, stat_sem, score_sem,
):
    me = lax.axis_index("dp")
    mp = lax.axis_index("mp")
    width = x.shape[1]
    blk = x.shape[0] // slots
    depth = w_query.shape[0]
    heads = w_query.shape[1] // HS
    share = out.shape[1]
    far = levels * blk

    def dp_at(step):
        return lax.rem(me + step, n_dp)

    def mp_at(step):
        return lax.rem(mp + step, n_mp)

    def kv_part(block, half):
        if half is None:
            return wkv.at[pl.ds(block * depth, depth), :]
        return wkv.at[pl.ds(block * depth + half * (depth // 2), depth // 2), :]

    def q_part(block, half):
        if half is None:
            return wq.at[pl.ds(block * depth, depth), :]
        return wq.at[pl.ds(block * depth + half * (depth // 2), depth // 2), :]

    rows_out = w_out.shape[0]

    def o_part(block, half):
        if half is None:
            return wo.at[block]
        return wo.at[block, pl.ds(half * (rows_out // 2), rows_out // 2), :]

    own_copies = [
        pltpu.make_async_copy(w_kv, kv_part(me, None), local_sem.at[0]),
        pltpu.make_async_copy(w_query, q_part(me, None), local_sem.at[1]),
        pltpu.make_async_copy(w_out, o_part(me, None), local_sem.at[2]),
    ]
    hidden_copies = [
        pltpu.make_async_copy(hidden.at[s], x.at[pl.ds(s * blk, blk), :], local_sem.at[4 + s])
        for s in range(slots)
    ]
    column = pl.multiple_of(mp * share, share)
    slice_copy = pltpu.make_async_copy(
        hidden.at[:, :, pl.ds(column, share)], own_hidden, local_sem.at[3]
    )
    for copy in own_copies + hidden_copies + [slice_copy]:
        copy.start()

    barrier = pltpu.get_barrier_semaphore()

    def greet_dp(step, carry):
        pl.semaphore_signal(barrier, inc=1, device_id=(dp_at(step), mp), device_id_type=MESH)
        return carry

    def greet_mp(step, carry):
        pl.semaphore_signal(barrier, inc=1, device_id=(me, mp_at(step)), device_id_type=MESH)
        return carry

    lax.fori_loop(1, n_dp, greet_dp, 0)
    lax.fori_loop(1, n_mp, greet_mp, 0)
    pl.semaphore_wait(barrier, n_dp - 1 + n_mp - 1)

    g_kv = Gather(
        kv_part, wkv.at[pl.ds(0, (n_dp - 1) * depth), :], send_sem.at[0], kv_sem, me, mp
    )
    g_q = Gather(q_part, wq.at[pl.ds(0, (n_dp - 1) * depth), :], send_sem.at[1], q_sem, me, mp)
    g_o = Gather(o_part, wo.at[pl.ds(0, n_dp - 1)], send_sem.at[2], o_sem, me, mp)

    own_copies[0].wait()
    g_kv.begin()

    def norm_segment(s):
        def rows_step(r, carry):
            rows = pl.ds(pl.multiple_of(s * blk + r * 16, 16), 16)
            floats = x[rows, :].astype(F32)
            meansq = jnp.mean(floats * floats, axis=-1, keepdims=True)
            scaled = floats * lax.rsqrt(meansq + 1e-05)
            x[rows, :] = (scaled * gain[...].astype(F32)).astype(BF16)
            return carry

        lax.fori_loop(0, blk // 16, rows_step, 0)

    kv_events = g_kv.events()
    for s in range(slots):
        hidden_copies[s].wait()
        norm_segment(s)
        kv_events[s]()
    for event in kv_events[slots:]:
        event()
    own_copies[1].wait()
    g_q.begin()

    group = slots // 2

    def kv_step(i, carry):
        rows = pl.ds(pl.multiple_of(i * group * blk, group * blk), group * blk)
        proj = jnp.dot(x[rows, :], wkv[...], preferred_element_type=F32)
        for r in range(group):
            piece = proj[r * blk : (r + 1) * blk]
            kv[i * group + r, :, :HS] = piece[:, :HS].astype(BF16)
            kv[i * group + r, :, HS:] = (piece[:, HS:] * V_SCALE).astype(BF16)
        return carry

    lax.fori_loop(0, slots // group, kv_step, 0)

    def a2a_send(step, carry):
        to = dp_at(step)
        kv_out[step] = kv[wanted[to]]
        start_copy(kv_out.at[step], kv_in.at[me], send_sem.at[3], a2a_sem.at[me], (to, mp))
        return carry

    lax.fori_loop(1, n_dp, a2a_send, 0)
    kv_in[me] = jnp.zeros(kv_in.shape[1:], BF16)

    q_events = g_q.events()
    for event in q_events:
        event()
    own_copies[2].wait()
    g_o.begin()

    q_scale = math.log2(math.e) / HS**0.5

    def q_step(i, carry):
        rows = pl.ds(pl.multiple_of(i * group * blk, group * blk), group * blk)
        proj = jnp.dot(x[rows, :], wq[...], preferred_element_type=F32) * q_scale
        for r in range(group):
            for h in range(heads):
                piece = proj[r * blk : (r + 1) * blk, h * HS : (h + 1) * HS]
                q[i * group + r, h * blk : (h + 1) * blk, :] = piece.astype(BF16)
        return carry

    o_events = g_o.events()
    for event in o_events[:3]:
        event()
    lax.fori_loop(0, slots // group, q_step, 0)
    for event in o_events[3:5]:
        event()

    token = lax.broadcasted_iota(jnp.int32, (blk, HS), 0)

    def masked(block, count):
        floats = block.astype(F32)
        live = token < count
        return (
            jnp.where(live, floats[:, :HS], 0.0).astype(BF16),
            jnp.where(live, floats[:, HS:], 0.0).astype(BF16),
            jnp.where(live, 1.0, 0.0).astype(BF16),
        )

    def near_step(s, carry):
        key, val, ones = masked(kv[s], own_len[s])
        near_v[s, :, :HS] = val
        near_v[s, :, HS:] = ones
        score = lax.dot_general(
            q[s], key, (((1,), (1,)), ((), ())), preferred_element_type=F32
        )
        row = lax.broadcasted_iota(jnp.int32, score.shape, 0) & (blk - 1)
        col = lax.broadcasted_iota(jnp.int32, score.shape, 1)
        near_w[s] = jnp.where(col <= row, jnp.exp2(score), 0.0).astype(BF16)
        return carry

    lax.fori_loop(0, slots, near_step, 0)
    for event in o_events[5:]:
        event()

    def a2a_wait(step, carry):
        source = dp_at(step)
        await_recv(kv_in.at[source], send_sem.at[3], a2a_sem.at[source], (source, mp))
        return carry

    lax.fori_loop(1, n_dp, a2a_wait, 0)

    def far_step(j, carry):
        key, val, ones = masked(kv_in[src[j]], anc_len[j])
        rows = pl.ds(pl.multiple_of(j * blk, blk), blk)
        keys[rows, :] = key
        vals[rows, :HS] = val
        vals[rows, HS:] = ones
        return carry

    lax.fori_loop(0, levels, far_step, 0)

    stat[...] = jnp.zeros(stat.shape, F32)
    chunk = 512
    plus, minus = (me, mp_at(1)), (me, mp_at(n_mp - 1))
    half = blk // 2

    def compute(s):
        def score_step(j, carry):
            cols = pl.ds(pl.multiple_of(j * chunk, chunk), chunk)
            score = lax.dot_general(
                q[s], keys[cols, :], (((1,), (1,)), ((), ())), preferred_element_type=F32
            )
            far_w[:, cols] = jnp.exp2(score).astype(BF16)
            return carry

        lax.fori_loop(0, far // chunk, score_step, 0)
        both = jnp.dot(far_w[...], vals[...], preferred_element_type=F32)
        both = both + jnp.dot(near_w[s], near_v[s], preferred_element_type=F32)
        mean = both[:, :HS] * (1.0 / both[:, HS:]) * (1.0 / V_SCALE)
        for h in range(heads):
            attn[:, h * HS : (h + 1) * HS] = mean[h * blk : (h + 1) * blk].astype(BF16)

        def out_step(j, carry):
            to = mp_at(n_mp // 2 + j)
            per = share // wo.shape[2]
            weight = jnp.concatenate([wo[to * per + i] for i in range(per)], axis=1)
            result = jnp.dot(attn[...], weight, preferred_element_type=F32)
            part[s, to] = result.astype(BF16)
            return carry

        lax.fori_loop(0, n_mp, out_step, 0)

    def send_half(s):
        to = mp_at(n_mp // 2)
        start_copy(
            part.at[s, to, pl.ds(0, half), :], half_in.at[s, 0], send_sem.at[4],
            half_sem.at[2 * s], plus,
        )
        start_copy(
            part.at[s, to, pl.ds(half, half), :], half_in.at[s, 1], send_sem.at[4],
            half_sem.at[2 * s + 1], minus,
        )

    def pass_on(s, hop):
        for side, device in ((0, plus), (1, minus)):
            steps = n_mp // 2 - 1 - hop
            to = mp_at(steps if side == 0 else n_mp - steps)
            if hop == 0:
                await_recv(half_in.at[s, side], send_sem.at[4], half_sem.at[2 * s + side], device)
                rows = pl.ds(side * half, half)
                mine = part[s, to, rows, :].astype(F32)
                part[s, to, rows, :] = (mine + half_in[s, side].astype(F32)).astype(BF16)
            else:
                sem = full_sem.at[(2 * s + side) * 3 + hop - 1]
                await_recv(full_in.at[s, side, hop - 1], send_sem.at[4], sem, device)
                mine = part[s, to].astype(F32)
                part[s, to] = (mine + full_in[s, side, hop - 1].astype(F32)).astype(BF16)
            sem = full_sem.at[(2 * s + side) * 3 + hop]
            start_copy(part.at[s, to], full_in.at[s, side, hop], send_sem.at[4], sem, device)

    def finish(s):
        for side, device in ((0, plus), (1, minus)):
            sem = full_sem.at[(2 * s + side) * 3 + 2]
            await_recv(full_in.at[s, side, 2], send_sem.at[4], sem, device)
        total = part[s, mp].astype(F32) + full_in[s, 0, 2].astype(F32)
        total = total + full_in[s, 1, 2].astype(F32)
        result = (own_hidden[s].astype(F32) + total).astype(BF16)
        out[pl.ds(pl.multiple_of(s * blk, blk), blk), :] = result
        floats = result.astype(F32)
        weighted = floats * w_head[:, pl.ds(column, share)]
        floats = floats * floats
        for base, terms in ((0, floats), (8, weighted)):
            lanes = terms[:, :128]
            for i in range(1, share // 128):
                lanes = lanes + terms[:, i * 128 : (i + 1) * 128]
            stat[pl.ds(base + s, 1), :] = jnp.sum(lanes.T, axis=0, keepdims=True)

    slice_copy.wait()

    def stage(t, carry):
        for late, act in (
            (4, finish),
            (3, lambda s: pass_on(s, 2)),
            (2, lambda s: pass_on(s, 1)),
            (1, lambda s: pass_on(s, 0)),
        ):
            s = t - late

            @pl.when((s >= 0) & (s < slots))
            def _():
                act(s)

        @pl.when(t < slots)
        def _():
            compute(t)
            send_half(t)

        return carry

    lax.fori_loop(0, slots + 4, stage, 0)

    def stat_send(step, carry):
        start_copy(stat, stats.at[mp], send_sem.at[5], stat_sem.at[mp], (me, mp_at(step)))
        return carry

    def stat_wait(step, carry):
        source = mp_at(step)
        await_recv(stats.at[source], send_sem.at[5], stat_sem.at[source], (me, source))
        return carry

    lax.fori_loop(1, n_mp, stat_send, 0)
    stats[mp] = stat[...]
    lax.fori_loop(1, n_mp, stat_wait, 0)
    sums = jnp.sum(stats[...], axis=0)
    token_score = sums[8:] * lax.rsqrt(sums[:8] / width + 1e-05)
    place = lax.broadcasted_iota(jnp.int32, token_score.shape, 1)
    used = place < lens[...]
    node = jnp.sum(jnp.where(used, token_score, 0.0), axis=1, keepdims=True)
    node = jnp.broadcast_to(node, token_score.shape) / lens[...].astype(F32)
    scores[me] = jnp.broadcast_to(jnp.sum(node, axis=0, keepdims=True), node.shape)

    def score_send(step, carry):
        start_copy(
            scores.at[me], scores.at[me], send_sem.at[6], score_sem.at[me], (dp_at(step), mp)
        )
        return carry

    def score_wait(step, carry):
        source = dp_at(step)
        await_recv(scores.at[source], send_sem.at[6], score_sem.at[source], (source, mp))
        return carry

    lax.fori_loop(1, n_dp, score_send, 0)
    lax.fori_loop(1, n_dp, score_wait, 0)
    values[...] = node + jnp.sum(hits[...] * scores[...], axis=0)

    g_kv.end()
    g_q.end()
    g_o.end()
    await_send(kv_out.at[pl.ds(0, n_dp - 1)], send_sem.at[3], a2a_sem.at[0], plus)
    await_send(part.at[:, pl.ds(0, n_mp - 1)], send_sem.at[4], half_sem.at[0], plus)
    await_send(stats.at[pl.ds(0, n_mp - 1)], send_sem.at[5], stat_sem.at[0], plus)
    await_send(scores.at[pl.ds(0, n_dp - 1)], send_sem.at[6], score_sem.at[0], plus)


def on_device(hidden, norm_gain, w_query, w_kv, w_out, w_head, parents, lengths):
    slots, blk, width = hidden.shape
    n_dp, n_mp = lax.axis_size("dp"), lax.axis_size("mp")
    levels = parents.shape[1]
    depth, q_columns = w_query.shape
    heads = q_columns // HS
    share = width // n_mp
    me = lax.axis_index("dp")
    w_kv = w_kv.reshape(depth, -1)
    kv_columns = w_kv.shape[1]
    firsts = parents.reshape(n_dp, slots, levels)[:, 0, :]
    mine_hit = (firsts >= me * slots) & (firsts < (me + 1) * slots)
    wanted = jnp.sum(jnp.where(mine_hit, firsts - me * slots, 0), axis=1).astype(jnp.int32)
    chain = lax.dynamic_index_in_dim(firsts, me, 0, keepdims=False)
    safe = jnp.maximum(chain, 0)
    anc_len = jnp.where(chain >= 0, jnp.take(lengths, safe), 0)
    src = safe // slots
    own_len = lax.dynamic_slice_in_dim(lengths, me * slots, slots)
    lens = jnp.concatenate([own_len, jnp.ones((8 - slots,), jnp.int32)])
    lens = jnp.broadcast_to(lens[:, None], (8, 128))
    own_nodes = me * slots + jnp.arange(8, dtype=jnp.int32)
    hits = jnp.any(firsts[:, None, :] == own_nodes[None, :, None], axis=2)
    hits = jnp.broadcast_to(hits.astype(F32)[:, :, None], (n_dp, 8, 128))
    any_space = pl.BlockSpec(memory_space=pl.ANY)
    vmem = pl.BlockSpec(memory_space=pltpu.VMEM)
    smem = pl.BlockSpec(memory_space=pltpu.SMEM)
    dma = pltpu.SemaphoreType.DMA
    far = levels * blk
    layer, values = pl.pallas_call(
        functools.partial(kernel, n_dp, n_mp, slots, levels),
        out_shape=(
            jax.ShapeDtypeStruct((slots * blk, share), BF16),
            jax.ShapeDtypeStruct((8, 128), F32),
        ),
        in_specs=[any_space, vmem, any_space, any_space, any_space, vmem]
        + [smem] * 4
        + [vmem] * 2,
        out_specs=(vmem, vmem),
        scratch_shapes=[
            pltpu.VMEM((slots * blk, width), BF16),
            pltpu.VMEM((slots, blk, share), BF16),
            pltpu.VMEM((width, q_columns), BF16),
            pltpu.VMEM((width, kv_columns), BF16),
            pltpu.VMEM((n_dp,) + w_out.shape, BF16),
            pltpu.VMEM((slots, heads * blk, HS), BF16),
            pltpu.VMEM((slots, blk, kv_columns), BF16),
            pltpu.VMEM((n_dp, blk, kv_columns), BF16),
            pltpu.VMEM((n_dp, blk, kv_columns), BF16),
            pltpu.VMEM((far, HS), BF16),
            pltpu.VMEM((far, 2 * HS), BF16),
            pltpu.VMEM((slots, blk, 2 * HS), BF16),
            pltpu.VMEM((slots, heads * blk, blk), BF16),
            pltpu.VMEM((heads * blk, far), BF16),
            pltpu.VMEM((blk, q_columns), BF16),
            pltpu.VMEM((slots, n_mp, blk, share), BF16),
            pltpu.VMEM((slots, 2, blk // 2, share), BF16),
            pltpu.VMEM((slots, 2, 3, blk, share), BF16),
            pltpu.VMEM((16, 128), F32),
            pltpu.VMEM((n_mp, 16, 128), F32),
            pltpu.VMEM((n_dp, 8, 128), F32),
            dma((4 + slots,)),
            dma((7,)),
            dma((36,)),
            dma((36,)),
            dma((36,)),
            dma((n_dp,)),
            dma((2 * slots,)),
            dma((6 * slots,)),
            dma((n_mp,)),
            dma((n_dp,)),
        ],
        compiler_params=pltpu.CompilerParams(
            collective_id=0, has_side_effects=True, vmem_limit_bytes=60 * 1024 * 1024
        ),
    )(
        hidden, norm_gain.reshape(1, width), w_query, w_kv, w_out, w_head.reshape(1, width),
        wanted, src, anc_len, own_len, lens, hits,
    )
    return layer.reshape(slots, blk, share), values[:slots, 0]


def solution(mesh):
    in_specs = (
        P("dp", None, None),
        P(),
        P("dp", "mp"),
        P("dp", None, "mp"),
        P("mp", "dp"),
        P(),
        P(),
        P(),
    )
    out_specs = (P("dp", None, "mp"), P("dp"))
    return jax.shard_map(
        on_device, mesh=mesh, in_specs=in_specs, out_specs=out_specs, check_vma=False
    )
```

```python
import functools
import math

import jax
import jax.numpy as jnp
from jax import lax
from jax.experimental import pallas as pl
from jax.experimental.pallas import tpu as pltpu
from jax.sharding import PartitionSpec as P

HS = 128
V_SCALE = 2.0**-10
F32 = jnp.float32
BF16 = jnp.bfloat16
MESH = pl.DeviceIdType.MESH


def start_copy(src, dst, send_sem, recv_sem, device):
    pltpu.make_async_remote_copy(
        src_ref=src, dst_ref=dst, send_sem=send_sem, recv_sem=recv_sem,
        device_id=device, device_id_type=MESH,
    ).start()


def await_recv(ref, send_sem, recv_sem, device):
    pltpu.make_async_remote_copy(
        src_ref=ref, dst_ref=ref, send_sem=send_sem, recv_sem=recv_sem,
        device_id=device, device_id_type=MESH,
    ).wait_recv()


def await_send(ref, send_sem, recv_sem, device):
    pltpu.make_async_remote_copy(
        src_ref=ref, dst_ref=ref, send_sem=send_sem, recv_sem=recv_sem,
        device_id=device, device_id_type=MESH,
    ).wait_send()


class Gather:
    def __init__(self, whole, send_sems, sems, me, mp):
        self.whole, self.send_sems, self.sems = whole, send_sems, sems
        self.mp = mp
        self.core = lax.rem(me, 2)
        self.x = lax.rem(lax.div(me, 2), 4)
        self.y = lax.div(me, 8)
        self.sibling = me + 1 - 2 * self.core

    def device(self, first, second):
        on_x = jnp.where(self.core == 0, first, second)
        on_y = jnp.where(self.core == 0, second, first)
        return lax.rem(self.y + on_y, 4) * 8 + lax.rem(self.x + on_x, 4) * 2 + self.core

    def block(self, back):
        on_x = jnp.where(self.core == 0, 4 - back, 0)
        on_y = jnp.where(self.core == 0, 0, 4 - back)
        return self.whole.at[lax.rem(self.y + on_y, 4), lax.rem(self.x + on_x, 4), self.core]

    def line(self, core, back):
        if core == 0:
            return self.whole.at[lax.rem(self.y + 4 - back, 4), :, 0]
        return self.whole.at[:, lax.rem(self.x + 4 - back, 4), 1]

    def per_core(self, act):
        for core in range(2):
            @pl.when(self.core == core)
            def _():
                act(core)

    def copy(self, ref, sem, to):
        return pltpu.make_async_remote_copy(
            src_ref=ref, dst_ref=ref, send_sem=self.send_sems.at[sem],
            recv_sem=self.sems.at[sem], device_id=(to, self.mp), device_id_type=MESH,
        )

    def begin(self):
        for step in (1, 3, 2):
            self.copy(self.block(0), step - 1, self.device(step, 0)).start()

    def first_done(self):
        for step in (1, 3, 2):
            self.copy(self.block(step), step - 1, self.sibling).wait_recv()

        def act(core):
            for step in (1, 3, 2):
                self.copy(self.line(core, 0), 2 + step, self.device(0, step)).start()
            self.copy(self.line(core, 0), 6, self.sibling).start()

        self.per_core(act)

    def second_done(self):
        def act(core):
            for step in (1, 3, 2):
                self.copy(self.line(core, step), 2 + step, self.sibling).wait_recv()
                self.copy(self.line(core, step), 6 + step, self.sibling).start()

        self.per_core(act)

    def all_done(self):
        def act(core):
            for step in (0, 1, 3, 2):
                self.copy(self.line(1 - core, step), 6 + step, self.sibling).wait_recv()

        self.per_core(act)

    def end(self):
        def act(core):
            for step in range(3, 10):
                self.copy(self.line(core, 0), step, self.sibling).wait_send()

        for step in range(3):
            self.copy(self.block(0), step, self.sibling).wait_send()
        self.per_core(act)


def kernel(
    n_dp, n_mp, slots, levels,
    hidden, gain, w_query, w_kv, w_out, w_head, parents, lengths,
    out, values,
    x, own_hidden, wq, wkv, wo, kv_own, gains, q, kv, kv_out, kv_in, keys, vals, near_v, near_w, far_w,
    attn, partial, stat, stats, scores, wanted,
    local_sem, kv_send, q_send, o_send, kv_sem, q_sem, o_sem, sort_sem, send_sem, a2a_sem,
    attn_sem, stat_sem, score_sem,
):
    me = lax.axis_index("dp")
    mp = lax.axis_index("mp")
    width = x.shape[1]
    blk = x.shape[0] // slots
    heads = wq.shape[-1] // HS
    share = out.shape[1]
    far = levels * blk
    core = lax.rem(me, 2)
    chip_x = lax.rem(lax.div(me, 2), 4)
    chip_y = lax.div(me, 8)
    first_node = me * slots

    def dp_at(step):
        return lax.rem(me + step, n_dp)

    def mp_at(step):
        return lax.rem(mp + step, n_mp)

    sort_to = (lax.rem(me, 4) * 8 + mp, lax.div(me, 4))
    sort_from = (mp * 4 + lax.div(me, 8), lax.rem(me, 8))
    stays = (sort_to[0] == me) & (sort_to[1] == mp)

    kv_copy = pltpu.make_async_copy(w_kv, kv_own, local_sem.at[0])
    q_copy = pltpu.make_async_copy(w_query, wq.at[chip_y, chip_x, core], local_sem.at[1])
    hidden_copies = [
        pltpu.make_async_copy(hidden.at[s], x.at[pl.ds(s * blk, blk), :], local_sem.at[4 + s])
        for s in range(slots)
    ]
    column = pl.multiple_of(mp * share, share)
    slice_copy = pltpu.make_async_copy(
        hidden.at[:, :, pl.ds(column, share)], own_hidden, local_sem.at[3]
    )
    kv_copy.start()
    for copy in hidden_copies:
        copy.start()
    q_copy.start()
    slice_copy.start()

    barrier = pltpu.get_barrier_semaphore()

    def greet(device):
        pl.semaphore_signal(barrier, inc=1, device_id=device, device_id_type=MESH)

    def greet_dp(step, carry):
        greet((dp_at(step), mp))
        return carry

    def greet_mp(step, carry):
        greet((me, mp_at(step)))
        return carry

    lax.fori_loop(1, n_dp, greet_dp, 0)
    lax.fori_loop(1, n_mp, greet_mp, 0)

    @pl.when(jnp.logical_not(stays))
    def _():
        greet(sort_to)
        greet(sort_from)

    g_kv = Gather(wkv, kv_send, kv_sem, me, mp)
    g_q = Gather(wq, q_send, q_sem, me, mp)
    g_o = Gather(wo, o_send, o_sem, me, mp)

    for i in range(width // HS):
        gains[:, i * HS : (i + 1) * HS] = gain[i : i + 1, :].astype(F32)

    def norm_segment(s):
        hidden_copies[s].wait()

        def rows_step(r, carry):
            rows = pl.ds(pl.multiple_of(s * blk + r * 16, 16), 16)
            floats = x[rows, :].astype(F32)
            meansq = jnp.mean(floats * floats, axis=-1, keepdims=True)
            scaled = floats * lax.rsqrt(meansq + 1e-05)
            x[rows, :] = (scaled * gains[...]).astype(BF16)
            return carry

        lax.fori_loop(0, blk // 16, rows_step, 0)

    kv_copy.wait()
    wkv[chip_y, chip_x, core, :, :HS] = kv_own[:, 0, :]
    wkv[chip_y, chip_x, core, :, HS:] = kv_own[:, 1, :]
    norm_segment(0)
    norm_segment(1)
    pl.semaphore_wait(barrier, jnp.where(stays, n_dp + n_mp - 2, n_dp + n_mp))

    g_kv.begin()
    norm_segment(2)
    norm_segment(3)
    g_kv.first_done()
    q_copy.wait()
    g_q.begin()
    norm_segment(4)
    norm_segment(5)

    def want_step(d, carry):
        slot = jnp.int32(-1)
        for j in range(levels):
            place = parents[j, d * slots] - first_node
            slot = jnp.where((place >= 0) & (place < slots), place, slot)
        wanted[d] = slot
        return carry

    lax.fori_loop(0, n_dp, want_step, 0)
    g_kv.second_done()
    g_q.first_done()
    g_kv.all_done()

    group = slots // 2

    def kv_step(i, carry):
        rows = pl.ds(pl.multiple_of(i * group * blk, group * blk), group * blk)
        weight = wkv[...].reshape(width, 2 * HS)
        proj = jnp.dot(x[rows, :], weight, preferred_element_type=F32)
        for r in range(group):
            piece = proj[r * blk : (r + 1) * blk]
            kv[i * group + r, :, :HS] = piece[:, :HS].astype(BF16)
            kv[i * group + r, :, HS:] = (piece[:, HS:] * V_SCALE).astype(BF16)
        return carry

    lax.fori_loop(0, slots // group, kv_step, 0)

    order = ((1, 0), (3, 0), (0, 1), (0, 3), (2, 0), (0, 2), (1, 1), (3, 3))
    order += ((1, 3), (3, 1), (2, 1), (1, 2), (2, 3), (3, 2), (2, 2), (0, 0))
    steps = [(dx, dy, 0) for dx, dy in order[:-1]] + [(dx, dy, 1) for dx, dy in order]
    for i, (dx, dy, flip) in enumerate(steps):
        to = lax.rem(chip_y + dy, 4) * 8 + lax.rem(chip_x + dx, 4) * 2 + lax.rem(core + flip, 2)
        kv_out[i] = kv[jnp.maximum(wanted[to], 0)]
        start_copy(kv_out.at[i], kv_in.at[me], send_sem.at[0], a2a_sem.at[me], (to, mp))
    kv_in[me] = jnp.zeros(kv_in.shape[1:], BF16)

    sort_slot = wo.at[lax.rem(me, 4), lax.div(mp, 2), lax.rem(mp, 2)]
    local_sort = pltpu.make_async_copy(w_out, sort_slot, local_sem.at[2])

    @pl.when(stays)
    def _():
        local_sort.start()

    @pl.when(jnp.logical_not(stays))
    def _():
        start_copy(w_out, sort_slot, sort_sem.at[0], sort_sem.at[1], sort_to)

    g_q.second_done()
    g_q.all_done()

    q_scale = math.log2(math.e) / HS**0.5

    def q_step(i, carry):
        rows = pl.ds(pl.multiple_of(i * group * blk, group * blk), group * blk)
        weight = wq[...].reshape(width, heads * HS)
        proj = jnp.dot(x[rows, :], weight, preferred_element_type=F32) * q_scale
        for r in range(group):
            for h in range(heads):
                piece = proj[r * blk : (r + 1) * blk, h * HS : (h + 1) * HS]
                q[i * group + r, h * blk : (h + 1) * blk, :] = piece.astype(BF16)
        return carry

    lax.fori_loop(0, slots // group, q_step, 0)

    token = lax.broadcasted_iota(jnp.int32, (blk, HS), 0)

    def masked(block, count):
        floats = block.astype(F32)
        live = token < count
        return (
            jnp.where(live, floats[:, :HS], 0.0).astype(BF16),
            jnp.where(live, floats[:, HS:], 0.0).astype(BF16),
            jnp.where(live, 1.0, 0.0).astype(BF16),
        )

    def near_step(s, carry):
        key, val, ones = masked(kv[s], lengths[first_node + s])
        near_v[s, :, :HS] = val
        near_v[s, :, HS:] = ones
        score = lax.dot_general(
            q[s], key, (((1,), (1,)), ((), ())), preferred_element_type=F32
        )
        row = lax.broadcasted_iota(jnp.int32, score.shape, 0) & (blk - 1)
        col = lax.broadcasted_iota(jnp.int32, score.shape, 1)
        near_w[s] = jnp.where(col <= row, jnp.exp2(score), 0.0).astype(BF16)
        return carry

    lax.fori_loop(0, slots, near_step, 0)
    stat[...] = jnp.zeros(stat.shape, F32)
    slice_copy.wait()
    g_kv.end()

    def a2a_wait(step, carry):
        source = dp_at(step)
        await_recv(kv_in.at[source], send_sem.at[0], a2a_sem.at[source], (source, mp))
        return carry

    lax.fori_loop(1, n_dp, a2a_wait, 0)

    @pl.when(stays)
    def _():
        local_sort.wait()

    @pl.when(jnp.logical_not(stays))
    def _():
        own_slot = wo.at[chip_y, chip_x, core]
        await_recv(own_slot, sort_sem.at[0], sort_sem.at[1], sort_from)

    g_o.begin()

    def far_step(j, carry):
        node = parents[j, first_node]
        safe = jnp.maximum(node, 0)
        count = jnp.where(node >= 0, lengths[safe], 0)
        key, val, ones = masked(kv_in[lax.div(safe, slots)], count)
        rows = pl.ds(pl.multiple_of(j * blk, blk), blk)
        keys[rows, :] = key
        vals[rows, :HS] = val
        vals[rows, HS:] = ones
        return carry

    lax.fori_loop(0, levels, far_step, 0)

    chunk = 512
    plus, minus = (me, mp_at(1)), (me, mp_at(n_mp - 1))
    sides = ((0, plus, n_mp - 1), (1, minus, 1))
    half = blk // 2

    def attend(s):
        def score_step(j, carry):
            cols = pl.ds(pl.multiple_of(j * chunk, chunk), chunk)
            score = lax.dot_general(
                q[s], keys[cols, :], (((1,), (1,)), ((), ())), preferred_element_type=F32
            )
            far_w[:, cols] = jnp.exp2(score).astype(BF16)
            return carry

        lax.fori_loop(0, far // chunk, score_step, 0)
        both = jnp.dot(far_w[...], vals[...], preferred_element_type=F32)
        both = both + jnp.dot(near_w[s], near_v[s], preferred_element_type=F32)
        mean = both[:, :HS] * (1.0 / both[:, HS:]) * (1.0 / V_SCALE)
        for h in range(heads):
            attn[s, mp, :, h * HS : (h + 1) * HS] = mean[h * blk : (h + 1) * blk].astype(BF16)

    def attn_part(s, side, hop):
        source = mp_at((n_mp - hop) if side == 0 else hop)
        if hop == n_mp // 2:
            return attn.at[s, source, pl.ds(side * half, half), :]
        return attn.at[s, source]

    def attn_sem_at(s, side, hop):
        return attn_sem.at[(s * 2 + side) * (n_mp // 2) + hop - 1]

    def send_on(s, hop):
        for side, device, _ in sides:
            if hop > 0:
                ref = attn_part(s, side, hop)
                await_recv(ref, send_sem.at[1], attn_sem_at(s, side, hop), device)
            source = mp_at((n_mp - hop) if side == 0 else hop)
            ref = attn.at[s, source]
            if hop + 1 == n_mp // 2:
                ref = attn.at[s, source, pl.ds(side * half, half), :]
            start_copy(ref, ref, send_sem.at[1], attn_sem_at(s, side, hop + 1), device)

    def attend_step(s, carry):
        attend(s)
        send_on(s, 0)

        @pl.when(s == 1)
        def _():
            g_o.first_done()

        return carry

    lax.fori_loop(0, slots, attend_step, 0)
    for s in range(slots):
        send_on(s, 1)
    g_o.second_done()
    for s in range(slots):
        send_on(s, 2)
    g_o.all_done()

    def weight_at(sources, pair):
        cols = []
        for j in (2 * pair, 2 * pair + 1):
            rows = [wo[j, lax.div(m, 2), lax.rem(m, 2)] for m in sources]
            cols.append(jnp.concatenate(rows, axis=0) if len(rows) > 1 else rows[0])
        return jnp.concatenate(cols, axis=1)

    opposite = mp_at(n_mp // 2)
    others = [mp_at(i) for i in range(n_mp) if i != n_mp // 2]

    def most(s, carry):
        send_on(s, 3)
        rows = jnp.concatenate([attn[s, m] for m in others], axis=1)
        for pair in range(2):
            cols = slice(pair * 2 * HS, (pair + 1) * 2 * HS)
            partial[s, :, cols] = jnp.dot(
                rows, weight_at(others, pair), preferred_element_type=F32
            )
        return carry

    lax.fori_loop(0, slots, most, 0)

    def finish(s, carry):
        for side, device, _ in sides:
            ref = attn_part(s, side, n_mp // 2)
            await_recv(ref, send_sem.at[1], attn_sem_at(s, side, n_mp // 2), device)
        weight = jnp.concatenate([weight_at([opposite], pair) for pair in range(2)], axis=1)
        total = partial[s] + jnp.dot(attn[s, opposite], weight, preferred_element_type=F32)
        result = (own_hidden[s].astype(F32) + total).astype(BF16)
        out[pl.ds(pl.multiple_of(s * blk, blk), blk), :] = result
        floats = result.astype(F32)
        heads_at = mp * (share // HS)
        head = jnp.concatenate(
            [w_head[pl.ds(heads_at + i, 1), :] for i in range(share // HS)], axis=1
        )
        weighted = floats * head
        floats = floats * floats
        for base, terms in ((0, floats), (8, weighted)):
            lanes = terms[:, :HS]
            for i in range(1, share // HS):
                lanes = lanes + terms[:, i * HS : (i + 1) * HS]
            stat[pl.ds(base + s, 1), :] = jnp.sum(lanes.T, axis=0, keepdims=True)
        return carry

    lax.fori_loop(0, slots, finish, 0)

    def stat_send(step, carry):
        start_copy(stat, stats.at[mp], send_sem.at[2], stat_sem.at[mp], (me, mp_at(step)))
        return carry

    def stat_wait(step, carry):
        source = mp_at(step)
        await_recv(stats.at[source], send_sem.at[2], stat_sem.at[source], (me, source))
        return carry

    lax.fori_loop(1, n_mp, stat_send, 0)
    stats[mp] = stat[...]
    place = lax.broadcasted_iota(jnp.int32, (8, 128), 1)
    row = lax.broadcasted_iota(jnp.int32, (8, 128), 0)
    lens = jnp.ones((8, 128), jnp.int32)
    for s in range(slots):
        lens = jnp.where(row == s, lengths[first_node + s], lens)
    lax.fori_loop(1, n_mp, stat_wait, 0)
    sums = jnp.sum(stats[...], axis=0)
    token_score = sums[8:] * lax.rsqrt(sums[:8] / width + 1e-05)
    node = jnp.sum(jnp.where(place < lens, token_score, 0.0), axis=1, keepdims=True)
    node = jnp.broadcast_to(node, token_score.shape) / lens.astype(F32)
    scores[me] = jnp.broadcast_to(jnp.sum(node, axis=0, keepdims=True), node.shape)

    def score_send(step, carry):
        start_copy(
            scores.at[me], scores.at[me], send_sem.at[3], score_sem.at[me], (dp_at(step), mp)
        )
        return carry

    def score_wait(step, carry):
        source = dp_at(step)
        await_recv(scores.at[source], send_sem.at[3], score_sem.at[source], (source, mp))
        return carry

    lax.fori_loop(1, n_dp, score_send, 0)

    g_q.end()
    g_o.end()

    @pl.when(jnp.logical_not(stays))
    def _():
        await_send(wo.at[chip_y, chip_x, core], sort_sem.at[0], sort_sem.at[1], sort_to)

    await_send(kv_out.at[pl.ds(0, n_dp - 1)], send_sem.at[0], a2a_sem.at[0], plus)
    await_send(attn.at[:, pl.ds(0, n_mp - 1)], send_sem.at[1], attn_sem.at[0], plus)
    await_send(stats.at[pl.ds(0, n_mp - 1)], send_sem.at[2], stat_sem.at[0], plus)
    lax.fori_loop(1, n_dp, score_wait, 0)

    def add_step(d, total):
        return total + jnp.where(row == wanted[d], scores[d], 0.0)

    values[...] = lax.fori_loop(0, n_dp, add_step, node)
    await_send(scores.at[pl.ds(0, n_dp - 1)], send_sem.at[3], score_sem.at[0], plus)


def on_device(hidden, norm_gain, w_query, w_kv, w_out, w_head, parents, lengths):
    slots, blk, width = hidden.shape
    n_dp, n_mp = lax.axis_size("dp"), lax.axis_size("mp")
    levels = parents.shape[1]
    depth, q_columns = w_query.shape
    heads = q_columns // HS
    share = width // n_mp
    any_space = pl.BlockSpec(memory_space=pl.ANY)
    vmem = pl.BlockSpec(memory_space=pltpu.VMEM)
    smem = pl.BlockSpec(memory_space=pltpu.SMEM)
    dma = pltpu.SemaphoreType.DMA
    far = levels * blk
    layer, values = pl.pallas_call(
        functools.partial(kernel, n_dp, n_mp, slots, levels),
        out_shape=(
            jax.ShapeDtypeStruct((slots * blk, share), BF16),
            jax.ShapeDtypeStruct((8, 128), F32),
        ),
        in_specs=[any_space, vmem, any_space, any_space, any_space, vmem, smem, smem],
        out_specs=(vmem, vmem),
        scratch_shapes=[
            pltpu.VMEM((slots * blk, width), BF16),
            pltpu.VMEM((slots, blk, share), BF16),
            pltpu.VMEM((4, 4, 2, depth, q_columns), BF16),
            pltpu.VMEM((4, 4, 2, depth, 2 * HS), BF16),
            pltpu.VMEM((4, 4, 2) + w_out.shape, BF16),
            pltpu.VMEM(w_kv.shape, BF16),
            pltpu.VMEM((1, width), F32),
            pltpu.VMEM((slots, heads * blk, HS), BF16),
            pltpu.VMEM((slots, blk, 2 * HS), BF16),
            pltpu.VMEM((n_dp, blk, 2 * HS), BF16),
            pltpu.VMEM((n_dp, blk, 2 * HS), BF16),
            pltpu.VMEM((far, HS), BF16),
            pltpu.VMEM((far, 2 * HS), BF16),
            pltpu.VMEM((slots, blk, 2 * HS), BF16),
            pltpu.VMEM((slots, heads * blk, blk), BF16),
            pltpu.VMEM((heads * blk, far), BF16),
            pltpu.VMEM((slots, n_mp, blk, q_columns), BF16),
            pltpu.VMEM((slots, blk, share), F32),
            pltpu.VMEM((16, 128), F32),
            pltpu.VMEM((n_mp, 16, 128), F32),
            pltpu.VMEM((n_dp, 8, 128), F32),
            pltpu.SMEM((n_dp,), jnp.int32),
            dma((4 + slots,)),
            dma((10,)),
            dma((10,)),
            dma((10,)),
            dma((10,)),
            dma((10,)),
            dma((10,)),
            dma((2,)),
            dma((4,)),
            dma((n_dp,)),
            dma((slots * n_mp,)),
            dma((n_mp,)),
            dma((n_dp,)),
        ],
        compiler_params=pltpu.CompilerParams(
            collective_id=0, has_side_effects=True, vmem_limit_bytes=60 * 1024 * 1024
        ),
    )(
        hidden, norm_gain.reshape(width // HS, HS), w_query, w_kv, w_out,
        w_head.reshape(width // HS, HS), parents.T, lengths,
    )
    return layer.reshape(slots, blk, share), values[:slots, 0]


def solution(mesh):
    in_specs = (
        P("dp", None, None),
        P(),
        P("dp", "mp"),
        P("dp", None, "mp"),
        P("mp", "dp"),
        P(),
        P(),
        P(),
    )
    out_specs = (P("dp", None, "mp"), P("dp"))
    return jax.shard_map(
        on_device, mesh=mesh, in_specs=in_specs, out_specs=out_specs, check_vma=False
    )
```

```python
import functools
import math

import jax
import jax.numpy as jnp
from jax import lax
from jax.experimental import pallas as pl
from jax.experimental.pallas import tpu as pltpu
from jax.sharding import PartitionSpec as P

HS = 128
V_SCALE = 2.0**-10
F32 = jnp.float32
BF16 = jnp.bfloat16
MESH = pl.DeviceIdType.MESH


def start_copy(src, dst, send_sem, recv_sem, device):
    pltpu.make_async_remote_copy(
        src_ref=src, dst_ref=dst, send_sem=send_sem, recv_sem=recv_sem,
        device_id=device, device_id_type=MESH,
    ).start()


def await_recv(ref, send_sem, recv_sem, device):
    pltpu.make_async_remote_copy(
        src_ref=ref, dst_ref=ref, send_sem=send_sem, recv_sem=recv_sem,
        device_id=device, device_id_type=MESH,
    ).wait_recv()


def await_send(ref, send_sem, recv_sem, device):
    pltpu.make_async_remote_copy(
        src_ref=ref, dst_ref=ref, send_sem=send_sem, recv_sem=recv_sem,
        device_id=device, device_id_type=MESH,
    ).wait_send()


class Gather:
    def __init__(self, whole, send_sems, sems, me, mp):
        self.whole, self.send_sems, self.sems = whole, send_sems, sems
        self.mp = mp
        self.core = lax.rem(me, 2)
        self.x = lax.rem(lax.div(me, 2), 4)
        self.y = lax.div(me, 8)
        self.sibling = me + 1 - 2 * self.core

    def device(self, first, second):
        on_x = jnp.where(self.core == 0, first, second)
        on_y = jnp.where(self.core == 0, second, first)
        return lax.rem(self.y + on_y, 4) * 8 + lax.rem(self.x + on_x, 4) * 2 + self.core

    def block(self, back):
        on_x = jnp.where(self.core == 0, 4 - back, 0)
        on_y = jnp.where(self.core == 0, 0, 4 - back)
        return self.whole.at[lax.rem(self.y + on_y, 4), lax.rem(self.x + on_x, 4), self.core]

    def line(self, core, back):
        if core == 0:
            return self.whole.at[lax.rem(self.y + 4 - back, 4), :, 0]
        return self.whole.at[:, lax.rem(self.x + 4 - back, 4), 1]

    def per_core(self, act):
        for core in range(2):
            @pl.when(self.core == core)
            def _():
                act(core)

    def copy(self, ref, sem, to):
        return pltpu.make_async_remote_copy(
            src_ref=ref, dst_ref=ref, send_sem=self.send_sems.at[sem],
            recv_sem=self.sems.at[sem], device_id=(to, self.mp), device_id_type=MESH,
        )

    def begin(self):
        for step in (1, 3, 2):
            self.copy(self.block(0), step - 1, self.device(step, 0)).start()

    def first_done(self):
        for step in (1, 3, 2):
            self.copy(self.block(step), step - 1, self.sibling).wait_recv()

        def act(core):
            for step in (1, 3, 2):
                self.copy(self.line(core, 0), 2 + step, self.device(0, step)).start()
            self.copy(self.line(core, 0), 6, self.sibling).start()

        self.per_core(act)

    def second_done(self):
        def act(core):
            for step in (1, 3, 2):
                self.copy(self.line(core, step), 2 + step, self.sibling).wait_recv()
                self.copy(self.line(core, step), 6 + step, self.sibling).start()

        self.per_core(act)

    def all_done(self):
        def act(core):
            for step in (0, 1, 3, 2):
                self.copy(self.line(1 - core, step), 6 + step, self.sibling).wait_recv()

        self.per_core(act)

    def end(self):
        def act(core):
            for step in range(3, 10):
                self.copy(self.line(core, 0), step, self.sibling).wait_send()

        for step in range(3):
            self.copy(self.block(0), step, self.sibling).wait_send()
        self.per_core(act)


def kernel(
    n_dp, n_mp, slots, levels,
    hidden, gain, w_query, w_kv, w_out, w_head, parents, lengths,
    out, values,
    x, own_hidden, wq, wkv, wo, kv_own, gains, q, kv, pair_out, pair_in, ring_out, ring_in, column_own,
    col_out, col_in, table, keys, vals, near_v, near_w, far_w,
    attn, partial, stat, stats, tallies, tally_in, hits,
    local_sem, kv_send, q_send, o_send, t_send, kv_sem, q_sem, o_sem, t_sem, sort_sem,
    route_send, route_sem, send_sem, attn_sem, stat_sem, tally_send, tally_sem,
):
    me = lax.axis_index("dp")
    mp = lax.axis_index("mp")
    width = x.shape[1]
    blk = x.shape[0] // slots
    heads = wq.shape[-1] // HS
    share = out.shape[1]
    far = levels * blk
    core = lax.rem(me, 2)
    chip_x = lax.rem(lax.div(me, 2), 4)
    chip_y = lax.div(me, 8)
    first_node = me * slots

    def mp_at(step):
        return lax.rem(mp + step, n_mp)

    sort_to = (lax.rem(me, 4) * 8 + mp, lax.div(me, 4))
    sort_from = (mp * 4 + lax.div(me, 8), lax.rem(me, 8))
    stays = (sort_to[0] == me) & (sort_to[1] == mp)

    kv_copy = pltpu.make_async_copy(w_kv, kv_own, local_sem.at[0])
    q_copy = pltpu.make_async_copy(w_query, wq.at[chip_y, chip_x, core], local_sem.at[1])
    hidden_copies = [
        pltpu.make_async_copy(hidden.at[s], x.at[pl.ds(s * blk, blk), :], local_sem.at[4 + s])
        for s in range(slots)
    ]
    column = pl.multiple_of(mp * share, share)
    slice_copy = pltpu.make_async_copy(
        hidden.at[:, :, pl.ds(column, share)], own_hidden, local_sem.at[3]
    )
    kv_copy.start()
    for copy in hidden_copies:
        copy.start()
    q_copy.start()
    slice_copy.start()

    barrier = pltpu.get_barrier_semaphore()

    def greet(device):
        pl.semaphore_signal(barrier, inc=1, device_id=device, device_id_type=MESH)

    def greet_mp(step, carry):
        greet((me, mp_at(step)))
        return carry

    g_kv = Gather(wkv, kv_send, kv_sem, me, mp)
    g_q = Gather(wq, q_send, q_sem, me, mp)
    g_o = Gather(wo, o_send, o_sem, me, mp)
    g_t = Gather(table, t_send, t_sem, me, mp)
    for step in (1, 3, 2):
        greet((g_kv.device(step, 0), mp))
        greet((g_kv.device(0, step), mp))
    greet((g_kv.sibling, mp))
    lax.fori_loop(1, n_mp, greet_mp, 0)

    @pl.when(jnp.logical_not(stays))
    def _():
        greet(sort_to)
        greet(sort_from)

    for i in range(width // HS):
        gains[:, i * HS : (i + 1) * HS] = gain[i : i + 1, :].astype(F32)

    def norm_segment(s):
        hidden_copies[s].wait()

        def rows_step(r, carry):
            rows = pl.ds(pl.multiple_of(s * blk + r * 16, 16), 16)
            floats = x[rows, :].astype(F32)
            meansq = jnp.mean(floats * floats, axis=-1, keepdims=True)
            scaled = floats * lax.rsqrt(meansq + 1e-05)
            x[rows, :] = (scaled * gains[...]).astype(BF16)
            return carry

        lax.fori_loop(0, blk // 16, rows_step, 0)

    kv_copy.wait()
    wkv[chip_y, chip_x, core, :, :HS] = kv_own[:, 0, :]
    wkv[chip_y, chip_x, core, :, HS:] = kv_own[:, 1, :]
    norm_segment(0)
    norm_segment(1)
    peers = 7 + n_mp - 1
    pl.semaphore_wait(barrier, jnp.where(stays, peers, peers + 2))

    g_kv.begin()
    norm_segment(2)
    norm_segment(3)
    g_kv.first_done()
    q_copy.wait()
    g_q.begin()
    norm_segment(4)
    norm_segment(5)

    g_kv.second_done()
    g_q.first_done()
    g_kv.all_done()

    group = slots // 2

    def kv_step(i, carry):
        rows = pl.ds(pl.multiple_of(i * group * blk, group * blk), group * blk)
        weight = wkv[...].reshape(width, 2 * HS)
        proj = jnp.dot(x[rows, :], weight, preferred_element_type=F32)
        for r in range(group):
            piece = proj[r * blk : (r + 1) * blk]
            kv[i * group + r, :, :HS] = piece[:, :HS].astype(BF16)
            kv[i * group + r, :, HS:] = (piece[:, HS:] * V_SCALE).astype(BF16)
        return carry

    lax.fori_loop(0, slots // group, kv_step, 0)

    f0 = jnp.where(core == 0, chip_x, chip_y)
    g0 = jnp.where(core == 0, chip_y, chip_x)
    f_mul = jnp.where(core == 0, 2, 8)
    g_mul = jnp.where(core == 0, 8, 2)

    def wanted(device):
        place = parents[0, device * slots] - first_node
        found = (place >= 0) & (place < slots)
        block = kv[jnp.clip(place, 0, slots - 1)]
        return jnp.where(found, block, jnp.zeros_like(block))

    def at4(value):
        return lax.rem(value, 4)

    for step in (2, 1, 3, 0):
        line = at4(g0 + step)
        for k in range(4):
            pair_out[step, k] = wanted(line * g_mul + k * f_mul + 1 - core)
        start_copy(
            pair_out.at[step], pair_in.at[step], route_send.at[step], route_sem.at[step],
            (g_kv.sibling, mp),
        )
    for step in (2, 1, 3, 0):
        await_recv(pair_in.at[step], route_send.at[step], route_sem.at[step], (g_kv.sibling, mp))
        line = at4(f0 + step)
        target = column_own if step == 0 else ring_out.at[step - 1]
        for k in range(4):
            target[k] = wanted(line * f_mul + k * g_mul + core) + pair_in[step, k]
        if step > 0:
            start_copy(
                ring_out.at[step - 1], ring_in.at[step - 1], route_send.at[3 + step],
                route_sem.at[3 + step], (g_kv.device(step, 0), mp),
            )

    def route_ring():
        for step in (1, 3, 2):
            await_recv(
                ring_in.at[step - 1], route_send.at[3 + step], route_sem.at[3 + step],
                (g_kv.sibling, mp),
            )

        def total(k):
            return column_own[k] + ring_in[0, k] + ring_in[1, k] + ring_in[2, k]

        for step in (2, 1, 3):
            col_out[step - 1] = total(at4(g0 + step))
            start_copy(
                col_out.at[step - 1], col_in.at[step - 1], route_send.at[6 + step],
                route_sem.at[6 + step], (g_kv.device(0, step), mp),
            )
        table[chip_y, chip_x, core] = total(g0)

    def route_column():
        for step in (1, 3, 2):
            await_recv(
                col_in.at[step - 1], route_send.at[6 + step], route_sem.at[6 + step],
                (g_kv.sibling, mp),
            )
        mine = table[chip_y, chip_x, core] + col_in[0] + col_in[1] + col_in[2]
        table[chip_y, chip_x, core] = mine
        g_t.begin()

    def route_end():
        for step in range(4):
            await_send(pair_out.at[step], route_send.at[step], route_sem.at[step], plus)
        for step in range(3):
            await_send(ring_out.at[step], route_send.at[4 + step], route_sem.at[4 + step], plus)
            await_send(col_out.at[step], route_send.at[7 + step], route_sem.at[7 + step], plus)

    plus, minus = (me, mp_at(1)), (me, mp_at(n_mp - 1))

    sort_slot = wo.at[lax.rem(me, 4), lax.div(mp, 2), lax.rem(mp, 2)]
    local_sort = pltpu.make_async_copy(w_out, sort_slot, local_sem.at[2])

    @pl.when(stays)
    def _():
        local_sort.start()

    @pl.when(jnp.logical_not(stays))
    def _():
        start_copy(w_out, sort_slot, sort_sem.at[0], sort_sem.at[1], sort_to)

    route_ring()
    g_q.second_done()
    route_column()
    g_q.all_done()

    q_scale = math.log2(math.e) / HS**0.5

    def q_step(i, carry):
        rows = pl.ds(pl.multiple_of(i * group * blk, group * blk), group * blk)
        weight = wq[...].reshape(width, heads * HS)
        proj = jnp.dot(x[rows, :], weight, preferred_element_type=F32) * q_scale
        for r in range(group):
            for h in range(heads):
                piece = proj[r * blk : (r + 1) * blk, h * HS : (h + 1) * HS]
                q[i * group + r, h * blk : (h + 1) * blk, :] = piece.astype(BF16)
        return carry

    lax.fori_loop(0, 1, q_step, 0)
    g_t.first_done()
    lax.fori_loop(1, slots // group, q_step, 0)

    token = lax.broadcasted_iota(jnp.int32, (blk, HS), 0)

    def masked(block, count):
        floats = block.astype(F32)
        live = token < count
        return (
            jnp.where(live, floats[:, :HS], 0.0).astype(BF16),
            jnp.where(live, floats[:, HS:], 0.0).astype(BF16),
            jnp.where(live, 1.0, 0.0).astype(BF16),
        )

    def near_step(s, carry):
        key, val, ones = masked(kv[s], lengths[first_node + s])
        near_v[s, :, :HS] = val
        near_v[s, :, HS:] = ones
        score = lax.dot_general(
            q[s], key, (((1,), (1,)), ((), ())), preferred_element_type=F32
        )
        row = lax.broadcasted_iota(jnp.int32, score.shape, 0) & (blk - 1)
        col = lax.broadcasted_iota(jnp.int32, score.shape, 1)
        near_w[s] = jnp.where(col <= row, jnp.exp2(score), 0.0).astype(BF16)
        return carry

    lax.fori_loop(0, slots, near_step, 0)
    stat[...] = jnp.zeros(stat.shape, F32)
    slice_copy.wait()
    g_kv.end()

    g_t.second_done()
    g_t.all_done()

    @pl.when(stays)
    def _():
        local_sort.wait()

    @pl.when(jnp.logical_not(stays))
    def _():
        own_slot = wo.at[chip_y, chip_x, core]
        await_recv(own_slot, sort_sem.at[0], sort_sem.at[1], sort_from)

    g_o.begin()

    def far_step(j, carry):
        node = parents[j, first_node]
        safe = jnp.maximum(node, 0)
        count = jnp.where(node >= 0, lengths[safe], 0)
        above = jnp.maximum(parents[jnp.maximum(j - 1, 0), first_node], 0)
        holder = jnp.where(j == 0, me, lax.div(above, slots))
        spot = table[lax.div(holder, 8), lax.div(lax.rem(holder, 8), 2), lax.rem(holder, 2)]
        key, val, ones = masked(spot, count)
        rows = pl.ds(pl.multiple_of(j * blk, blk), blk)
        keys[rows, :] = key
        vals[rows, :HS] = val
        vals[rows, HS:] = ones
        return carry

    lax.fori_loop(0, levels, far_step, 0)

    chunk = 512
    sides = ((0, plus, n_mp - 1), (1, minus, 1))
    half = blk // 2

    def attend(s):
        def score_step(j, carry):
            cols = pl.ds(pl.multiple_of(j * chunk, chunk), chunk)
            score = lax.dot_general(
                q[s], keys[cols, :], (((1,), (1,)), ((), ())), preferred_element_type=F32
            )
            far_w[:, cols] = jnp.exp2(score).astype(BF16)
            return carry

        lax.fori_loop(0, far // chunk, score_step, 0)
        both = jnp.dot(far_w[...], vals[...], preferred_element_type=F32)
        both = both + jnp.dot(near_w[s], near_v[s], preferred_element_type=F32)
        mean = both[:, :HS] * (1.0 / both[:, HS:]) * (1.0 / V_SCALE)
        for h in range(heads):
            attn[s, mp, :, h * HS : (h + 1) * HS] = mean[h * blk : (h + 1) * blk].astype(BF16)

    def attn_part(s, side, hop):
        source = mp_at((n_mp - hop) if side == 0 else hop)
        if hop == n_mp // 2:
            return attn.at[s, source, pl.ds(side * half, half), :]
        return attn.at[s, source]

    def attn_sem_at(s, side, hop):
        return attn_sem.at[(s * 2 + side) * (n_mp // 2) + hop - 1]

    def send_on(s, hop):
        for side, device, _ in sides:
            if hop > 0:
                ref = attn_part(s, side, hop)
                await_recv(ref, send_sem.at[0], attn_sem_at(s, side, hop), device)
            source = mp_at((n_mp - hop) if side == 0 else hop)
            ref = attn.at[s, source]
            if hop + 1 == n_mp // 2:
                ref = attn.at[s, source, pl.ds(side * half, half), :]
            start_copy(ref, ref, send_sem.at[0], attn_sem_at(s, side, hop + 1), device)

    def attend_step(s, carry):
        attend(s)
        send_on(s, 0)

        @pl.when(s == 1)
        def _():
            g_o.first_done()

        return carry

    lax.fori_loop(0, slots, attend_step, 0)
    for s in range(slots):
        send_on(s, 1)
    g_o.second_done()
    for s in range(slots):
        send_on(s, 2)
    g_o.all_done()

    row = lax.broadcasted_iota(jnp.int32, (8, 128), 0)
    place = lax.broadcasted_iota(jnp.int32, (8, 128), 1)

    def hit_step(d, total):
        slot = jnp.int32(-1)
        for j in range(levels):
            spot = parents[j, d * slots] - first_node
            slot = jnp.where((spot >= 0) & (spot < slots), spot, slot)
        return total + jnp.where((row == slot) & (place == d), 1.0, 0.0)

    hits[...] = lax.fori_loop(0, n_dp, hit_step, jnp.zeros((8, 128), F32))

    g_q.end()
    g_o.end()
    g_t.end()
    route_end()

    @pl.when(jnp.logical_not(stays))
    def _():
        await_send(wo.at[chip_y, chip_x, core], sort_sem.at[0], sort_sem.at[1], sort_to)

    def weight_at(sources, pair):
        cols = []
        for j in (2 * pair, 2 * pair + 1):
            rows = [wo[j, lax.div(m, 2), lax.rem(m, 2)] for m in sources]
            cols.append(jnp.concatenate(rows, axis=0) if len(rows) > 1 else rows[0])
        return jnp.concatenate(cols, axis=1)

    opposite = mp_at(n_mp // 2)
    others = [mp_at(i) for i in range(n_mp) if i != n_mp // 2]

    def most(s, carry):
        send_on(s, 3)
        rows = jnp.concatenate([attn[s, m] for m in others], axis=1)
        for pair in range(2):
            cols = slice(pair * 2 * HS, (pair + 1) * 2 * HS)
            partial[s, :, cols] = jnp.dot(
                rows, weight_at(others, pair), preferred_element_type=F32
            )
        return carry

    lax.fori_loop(0, slots, most, 0)

    def finish(s, carry):
        for side, device, _ in sides:
            ref = attn_part(s, side, n_mp // 2)
            await_recv(ref, send_sem.at[0], attn_sem_at(s, side, n_mp // 2), device)
        weight = jnp.concatenate([weight_at([opposite], pair) for pair in range(2)], axis=1)
        total = partial[s] + jnp.dot(attn[s, opposite], weight, preferred_element_type=F32)
        result = (own_hidden[s].astype(F32) + total).astype(BF16)
        out[pl.ds(pl.multiple_of(s * blk, blk), blk), :] = result
        floats = result.astype(F32)
        heads_at = mp * (share // HS)
        head = jnp.concatenate(
            [w_head[pl.ds(heads_at + i, 1), :] for i in range(share // HS)], axis=1
        )
        weighted = floats * head
        floats = floats * floats
        for base, terms in ((0, floats), (8, weighted)):
            lanes = terms[:, :HS]
            for i in range(1, share // HS):
                lanes = lanes + terms[:, i * HS : (i + 1) * HS]
            stat[pl.ds(base + s, 1), :] = jnp.sum(lanes.T, axis=0, keepdims=True)
        return carry

    lax.fori_loop(0, slots, finish, 0)

    def stat_send(step, carry):
        start_copy(stat, stats.at[mp], send_sem.at[1], stat_sem.at[mp], (me, mp_at(step)))
        return carry

    def stat_wait(step, carry):
        source = mp_at(step)
        await_recv(stats.at[source], send_sem.at[1], stat_sem.at[source], (me, source))
        return carry

    lax.fori_loop(1, n_mp, stat_send, 0)
    stats[mp] = stat[...]
    lens = jnp.ones((8, 128), jnp.int32)
    for s in range(slots):
        lens = jnp.where(row == s, lengths[first_node + s], lens)
    lax.fori_loop(1, n_mp, stat_wait, 0)
    sums = jnp.sum(stats[...], axis=0)
    token_score = sums[8:] * lax.rsqrt(sums[:8] / width + 1e-05)
    node = jnp.sum(jnp.where(place < lens, token_score, 0.0), axis=1, keepdims=True)
    node = jnp.broadcast_to(node, token_score.shape) / lens.astype(F32)
    own = jnp.broadcast_to(jnp.sum(node, axis=0, keepdims=True), node.shape)
    tallies[0] = jnp.where(place == me, own, 0.0)

    def tally(level, sems, devices):
        for sem, device in zip(sems, devices):
            start_copy(
                tallies.at[level], tally_in.at[sem], tally_send.at[sem], tally_sem.at[sem],
                (device, mp),
            )
        total = tallies[level]
        for sem, device in zip(sems, devices):
            await_recv(tally_in.at[sem], tally_send.at[sem], tally_sem.at[sem], (device, mp))
            total = total + tally_in[sem]
        tallies[level + 1] = total

    tally(0, (0,), (g_kv.sibling,))
    tally(1, (1, 2, 3), [g_kv.device(step, 0) for step in (1, 2, 3)])
    tally(2, (4, 5, 6), [g_kv.device(0, step) for step in (1, 2, 3)])
    below = jnp.sum(hits[...] * tallies[3], axis=1, keepdims=True)
    values[...] = node + below
    await_send(attn.at[:, pl.ds(0, n_mp - 1)], send_sem.at[0], attn_sem.at[0], plus)
    await_send(stats.at[pl.ds(0, n_mp - 1)], send_sem.at[1], stat_sem.at[0], plus)
    for sem in range(7):
        await_send(tallies.at[0], tally_send.at[sem], tally_sem.at[sem], plus)


def on_device(hidden, norm_gain, w_query, w_kv, w_out, w_head, parents, lengths):
    slots, blk, width = hidden.shape
    n_dp, n_mp = lax.axis_size("dp"), lax.axis_size("mp")
    levels = parents.shape[1]
    depth, q_columns = w_query.shape
    heads = q_columns // HS
    share = width // n_mp
    any_space = pl.BlockSpec(memory_space=pl.ANY)
    vmem = pl.BlockSpec(memory_space=pltpu.VMEM)
    smem = pl.BlockSpec(memory_space=pltpu.SMEM)
    dma = pltpu.SemaphoreType.DMA
    far = levels * blk
    layer, values = pl.pallas_call(
        functools.partial(kernel, n_dp, n_mp, slots, levels),
        out_shape=(
            jax.ShapeDtypeStruct((slots * blk, share), BF16),
            jax.ShapeDtypeStruct((8, 128), F32),
        ),
        in_specs=[any_space, vmem, any_space, any_space, any_space, vmem, smem, smem],
        out_specs=(vmem, vmem),
        scratch_shapes=[
            pltpu.VMEM((slots * blk, width), BF16),
            pltpu.VMEM((slots, blk, share), BF16),
            pltpu.VMEM((4, 4, 2, depth, q_columns), BF16),
            pltpu.VMEM((4, 4, 2, depth, 2 * HS), BF16),
            pltpu.VMEM((4, 4, 2) + w_out.shape, BF16),
            pltpu.VMEM(w_kv.shape, BF16),
            pltpu.VMEM((1, width), F32),
            pltpu.VMEM((slots, heads * blk, HS), BF16),
            pltpu.VMEM((slots, blk, 2 * HS), BF16),
            pltpu.VMEM((4, 4, blk, 2 * HS), BF16),
            pltpu.VMEM((4, 4, blk, 2 * HS), BF16),
            pltpu.VMEM((3, 4, blk, 2 * HS), BF16),
            pltpu.VMEM((3, 4, blk, 2 * HS), BF16),
            pltpu.VMEM((4, blk, 2 * HS), BF16),
            pltpu.VMEM((3, blk, 2 * HS), BF16),
            pltpu.VMEM((3, blk, 2 * HS), BF16),
            pltpu.VMEM((4, 4, 2, blk, 2 * HS), BF16),
            pltpu.VMEM((far, HS), BF16),
            pltpu.VMEM((far, 2 * HS), BF16),
            pltpu.VMEM((slots, blk, 2 * HS), BF16),
            pltpu.VMEM((slots, heads * blk, blk), BF16),
            pltpu.VMEM((heads * blk, far), BF16),
            pltpu.VMEM((slots, n_mp, blk, q_columns), BF16),
            pltpu.VMEM((slots, blk, share), F32),
            pltpu.VMEM((16, 128), F32),
            pltpu.VMEM((n_mp, 16, 128), F32),
            pltpu.VMEM((4, 8, 128), F32),
            pltpu.VMEM((7, 8, 128), F32),
            pltpu.VMEM((8, 128), F32),
            dma((4 + slots,)),
            dma((10,)),
            dma((10,)),
            dma((10,)),
            dma((10,)),
            dma((10,)),
            dma((10,)),
            dma((10,)),
            dma((10,)),
            dma((2,)),
            dma((10,)),
            dma((10,)),
            dma((2,)),
            dma((slots * n_mp,)),
            dma((n_mp,)),
            dma((7,)),
            dma((7,)),
        ],
        compiler_params=pltpu.CompilerParams(
            collective_id=0, has_side_effects=True, vmem_limit_bytes=60 * 1024 * 1024
        ),
    )(
        hidden, norm_gain.reshape(width // HS, HS), w_query, w_kv, w_out,
        w_head.reshape(width // HS, HS), parents.T, lengths,
    )
    return layer.reshape(slots, blk, share), values[:slots, 0]


def solution(mesh):
    in_specs = (
        P("dp", None, None),
        P(),
        P("dp", "mp"),
        P("dp", None, "mp"),
        P("mp", "dp"),
        P(),
        P(),
        P(),
    )
    out_specs = (P("dp", None, "mp"), P("dp"))
    return jax.shard_map(
        on_device, mesh=mesh, in_specs=in_specs, out_specs=out_specs, check_vma=False
    )
```

```python
import functools
import math

import jax
import jax.numpy as jnp
from jax import lax
from jax.experimental import pallas as pl
from jax.experimental.pallas import tpu as pltpu
from jax.sharding import PartitionSpec as P

HS = 128
V_SCALE = 2.0**-10
F32 = jnp.float32
BF16 = jnp.bfloat16
MESH = pl.DeviceIdType.MESH


def start_copy(src, dst, send_sem, recv_sem, device):
    pltpu.make_async_remote_copy(
        src_ref=src, dst_ref=dst, send_sem=send_sem, recv_sem=recv_sem,
        device_id=device, device_id_type=MESH,
    ).start()


def await_recv(ref, send_sem, recv_sem, device):
    pltpu.make_async_remote_copy(
        src_ref=ref, dst_ref=ref, send_sem=send_sem, recv_sem=recv_sem,
        device_id=device, device_id_type=MESH,
    ).wait_recv()


def await_send(ref, send_sem, recv_sem, device):
    pltpu.make_async_remote_copy(
        src_ref=ref, dst_ref=ref, send_sem=send_sem, recv_sem=recv_sem,
        device_id=device, device_id_type=MESH,
    ).wait_send()


class Gather:
    def __init__(self, whole, send_sems, sems, me, mp):
        self.whole, self.send_sems, self.sems = whole, send_sems, sems
        self.mp = mp
        self.core = lax.rem(me, 2)
        self.x = lax.rem(lax.div(me, 2), 4)
        self.y = lax.div(me, 8)
        self.sibling = me + 1 - 2 * self.core

    def device(self, first, second):
        on_x = jnp.where(self.core == 0, first, second)
        on_y = jnp.where(self.core == 0, second, first)
        return lax.rem(self.y + on_y, 4) * 8 + lax.rem(self.x + on_x, 4) * 2 + self.core

    def block(self, back):
        on_x = jnp.where(self.core == 0, 4 - back, 0)
        on_y = jnp.where(self.core == 0, 0, 4 - back)
        return self.whole.at[lax.rem(self.y + on_y, 4), lax.rem(self.x + on_x, 4), self.core]

    def line(self, core, back):
        if core == 0:
            return self.whole.at[lax.rem(self.y + 4 - back, 4), :, 0]
        return self.whole.at[:, lax.rem(self.x + 4 - back, 4), 1]

    def per_core(self, act):
        for core in range(2):
            @pl.when(self.core == core)
            def _():
                act(core)

    def copy(self, ref, sem, to):
        return pltpu.make_async_remote_copy(
            src_ref=ref, dst_ref=ref, send_sem=self.send_sems.at[sem],
            recv_sem=self.sems.at[sem], device_id=(to, self.mp), device_id_type=MESH,
        )

    def begin(self):
        for step in (1, 3, 2):
            self.copy(self.block(0), step - 1, self.device(step, 0)).start()

    def first_done(self):
        for step in (1, 3, 2):
            self.copy(self.block(step), step - 1, self.sibling).wait_recv()

        def act(core):
            for step in (1, 3, 2):
                self.copy(self.line(core, 0), 2 + step, self.device(0, step)).start()
            self.copy(self.line(core, 0), 6, self.sibling).start()

        self.per_core(act)

    def second_done(self):
        def act(core):
            for step in (1, 3, 2):
                self.copy(self.line(core, step), 2 + step, self.sibling).wait_recv()
                self.copy(self.line(core, step), 6 + step, self.sibling).start()

        self.per_core(act)

    def all_done(self):
        def act(core):
            for step in (0, 1, 3, 2):
                self.copy(self.line(1 - core, step), 6 + step, self.sibling).wait_recv()

        self.per_core(act)

    def end(self):
        def act(core):
            for step in range(3, 10):
                self.copy(self.line(core, 0), step, self.sibling).wait_send()

        for step in range(3):
            self.copy(self.block(0), step, self.sibling).wait_send()
        self.per_core(act)


def kernel(
    n_dp, n_mp, slots, levels,
    hidden, gain, w_query, w_kv, w_out, w_head, parents, lengths,
    out, values,
    x, own_hidden, wq, wkv, wo, kv_own, gains, q, kv, pair_out, pair_in, ring_out, ring_in, column_own,
    col_out, col_in, table, keys, vals, near_v, near_w, far_w,
    attn, far_out, far_in, partial, stat, stats, tallies, tally_in, hits,
    local_sem, kv_send, q_send, far_send, own_send, t_send, kv_sem, q_sem, far_sem, own_sem, t_sem, sort_send,
    sort_sem, route_send, route_sem, send_sem, attn_sem, cross_sem, stat_sem, tally_send, tally_sem,
):
    me = lax.axis_index("dp")
    mp = lax.axis_index("mp")
    width = x.shape[1]
    blk = x.shape[0] // slots
    heads = wq.shape[-1] // HS
    share = out.shape[1]
    far = levels * blk
    core = lax.rem(me, 2)
    chip_x = lax.rem(lax.div(me, 2), 4)
    chip_y = lax.div(me, 8)
    first_node = me * slots

    def mp_at(step):
        return lax.rem(mp + step, n_mp)

    def place_of(plane, cut):
        i = lax.rem(plane + n_mp - 2 * cut, n_mp)
        return lax.div(i, 4), lax.rem(i, 4)

    def plane_at(cut, side, j):
        return lax.rem(2 * cut + side * 4 + j, n_mp)

    halves = [place_of(mp, cut) for cut in range(2)]
    end_cut = jnp.where((halves[0][1] == 0) | (halves[0][1] == 3), 0, 1)
    end_half, end_j = place_of(mp, end_cut)
    outward = jnp.where(end_j == 3, 1, n_mp - 1)

    def sort_target(cut):
        columns = lax.div(me, 4)
        their_half, their_j = place_of(columns, cut)
        half, j = place_of(mp, cut)
        same = their_half == half
        across = jnp.where(their_j < 2, their_j, 3 - their_j)
        end = plane_at(cut, half, jnp.where(their_j < 2, 3, 0))
        block = jnp.where(same, cut, across) * 16 + j * 4 + lax.rem(me, 4)
        return (block, jnp.where(same, columns, end)), jnp.where(same, 0, 1)

    def sort_source(kind):
        which, j, column = lax.div(me, 16), lax.div(lax.rem(me, 16), 4), lax.rem(me, 4)
        if kind == 0:
            half = jnp.where(which == 0, halves[0][0], halves[1][0])
            return mp * 4 + column, plane_at(which, half, j)
        columns = lax.rem(mp + outward * (which + 1), n_mp)
        return columns * 4 + column, plane_at(end_cut, end_half, j)

    def is_me(device):
        return (device[0] == me) & (device[1] == mp)

    sort_to = [sort_target(cut) for cut in range(2)]
    sort_from = [sort_source(kind) for kind in range(2)]
    strangers = [device for device, _ in sort_to] + sort_from

    def wo_block(kind, block):
        return wo.at[kind, lax.div(block, 8), lax.div(lax.rem(block, 8), 2), lax.rem(block, 2)]

    kv_copy = pltpu.make_async_copy(w_kv, kv_own, local_sem.at[0])
    q_copy = pltpu.make_async_copy(w_query, wq.at[chip_y, chip_x, core], local_sem.at[1])
    hidden_copies = [
        pltpu.make_async_copy(hidden.at[s], x.at[pl.ds(s * blk, blk), :], local_sem.at[4 + s])
        for s in range(slots)
    ]
    column = pl.multiple_of(mp * share, share)
    slice_copy = pltpu.make_async_copy(
        hidden.at[:, :, pl.ds(column, share)], own_hidden, local_sem.at[3]
    )
    kv_copy.start()
    for copy in hidden_copies:
        copy.start()
    q_copy.start()
    slice_copy.start()

    barrier = pltpu.get_barrier_semaphore()

    def greet(device):
        pl.semaphore_signal(barrier, inc=1, device_id=device, device_id_type=MESH)

    def greet_mp(step, carry):
        greet((me, mp_at(step)))
        return carry

    g_kv = Gather(wkv, kv_send, kv_sem, me, mp)
    g_q = Gather(wq, q_send, q_sem, me, mp)
    g_far = Gather(wo.at[1], far_send, far_sem, me, mp)
    g_own = Gather(wo.at[0], own_send, own_sem, me, mp)
    g_t = Gather(table, t_send, t_sem, me, mp)
    for step in (1, 3, 2):
        greet((g_kv.device(step, 0), mp))
        greet((g_kv.device(0, step), mp))
    greet((g_kv.sibling, mp))
    lax.fori_loop(1, n_mp, greet_mp, 0)

    for stranger in strangers:
        @pl.when(jnp.logical_not(is_me(stranger)))
        def _():
            greet(stranger)

    for i in range(width // HS):
        gains[:, i * HS : (i + 1) * HS] = gain[i : i + 1, :].astype(F32)

    def norm_segment(s):
        hidden_copies[s].wait()

        def rows_step(r, carry):
            rows = pl.ds(pl.multiple_of(s * blk + r * 16, 16), 16)
            floats = x[rows, :].astype(F32)
            meansq = jnp.mean(floats * floats, axis=-1, keepdims=True)
            scaled = floats * lax.rsqrt(meansq + 1e-05)
            x[rows, :] = (scaled * gains[...]).astype(BF16)
            return carry

        lax.fori_loop(0, blk // 16, rows_step, 0)

    kv_copy.wait()
    wkv[chip_y, chip_x, core, :, :HS] = kv_own[:, 0, :]
    wkv[chip_y, chip_x, core, :, HS:] = kv_own[:, 1, :]
    norm_segment(0)
    norm_segment(1)
    peers = 7 + n_mp - 1
    for stranger in strangers:
        peers = peers + jnp.where(is_me(stranger), 0, 1)
    pl.semaphore_wait(barrier, peers)

    g_kv.begin()
    q_copy.wait()
    g_q.begin()
    norm_segment(2)
    norm_segment(3)
    g_kv.first_done()
    norm_segment(4)
    norm_segment(5)
    g_q.first_done()
    g_kv.second_done()
    g_kv.all_done()

    group = slots // 2

    def kv_step(i, carry):
        rows = pl.ds(pl.multiple_of(i * group * blk, group * blk), group * blk)
        weight = wkv[...].reshape(width, 2 * HS)
        proj = jnp.dot(x[rows, :], weight, preferred_element_type=F32)
        for r in range(group):
            piece = proj[r * blk : (r + 1) * blk]
            kv[i * group + r, :, :HS] = piece[:, :HS].astype(BF16)
            kv[i * group + r, :, HS:] = (piece[:, HS:] * V_SCALE).astype(BF16)
        return carry

    lax.fori_loop(0, slots // group, kv_step, 0)

    f0 = jnp.where(core == 0, chip_x, chip_y)
    g0 = jnp.where(core == 0, chip_y, chip_x)
    f_mul = jnp.where(core == 0, 2, 8)
    g_mul = jnp.where(core == 0, 8, 2)

    def wanted(device):
        place = parents[0, device * slots] - first_node
        found = (place >= 0) & (place < slots)
        block = kv[jnp.clip(place, 0, slots - 1)]
        return jnp.where(found, block, jnp.zeros_like(block))

    def at4(value):
        return lax.rem(value, 4)

    for step in (2, 1, 3, 0):
        line = at4(g0 + step)
        for k in range(4):
            pair_out[step, k] = wanted(line * g_mul + k * f_mul + 1 - core)
        start_copy(
            pair_out.at[step], pair_in.at[step], route_send.at[step], route_sem.at[step],
            (g_kv.sibling, mp),
        )
    for step in (2, 1, 3, 0):
        await_recv(pair_in.at[step], route_send.at[step], route_sem.at[step], (g_kv.sibling, mp))
        line = at4(f0 + step)
        target = column_own if step == 0 else ring_out.at[step - 1]
        for k in range(4):
            target[k] = wanted(line * f_mul + k * g_mul + core) + pair_in[step, k]
        if step > 0:
            start_copy(
                ring_out.at[step - 1], ring_in.at[step - 1], route_send.at[3 + step],
                route_sem.at[3 + step], (g_kv.device(step, 0), mp),
            )

    def route_ring():
        for step in (1, 3, 2):
            await_recv(
                ring_in.at[step - 1], route_send.at[3 + step], route_sem.at[3 + step],
                (g_kv.sibling, mp),
            )

        def total(k):
            return column_own[k] + ring_in[0, k] + ring_in[1, k] + ring_in[2, k]

        for step in (2, 1, 3):
            col_out[step - 1] = total(at4(g0 + step))
            start_copy(
                col_out.at[step - 1], col_in.at[step - 1], route_send.at[6 + step],
                route_sem.at[6 + step], (g_kv.device(0, step), mp),
            )
        table[chip_y, chip_x, core] = total(g0)

    def route_column():
        for step in (1, 3, 2):
            await_recv(
                col_in.at[step - 1], route_send.at[6 + step], route_sem.at[6 + step],
                (g_kv.sibling, mp),
            )
        mine = table[chip_y, chip_x, core] + col_in[0] + col_in[1] + col_in[2]
        table[chip_y, chip_x, core] = mine
        g_t.begin()

    def route_end():
        for step in range(4):
            await_send(pair_out.at[step], route_send.at[step], route_sem.at[step], plus)
        for step in range(3):
            await_send(ring_out.at[step], route_send.at[4 + step], route_sem.at[4 + step], plus)
            await_send(col_out.at[step], route_send.at[7 + step], route_sem.at[7 + step], plus)

    plus, minus = (me, mp_at(1)), (me, mp_at(n_mp - 1))

    route_ring()
    route_column()
    g_q.second_done()
    g_t.first_done()
    g_q.all_done()

    sort_local = [
        pltpu.make_async_copy(w_out, wo_block(kind, device[0]), local_sem.at[4 + slots + cut])
        for cut, (device, kind) in enumerate(sort_to)
    ]
    for cut, (device, kind) in enumerate(sort_to):
        @pl.when(is_me(device))
        def _():
            sort_local[cut].start()

        @pl.when(jnp.logical_not(is_me(device)))
        def _():
            start_copy(
                w_out, wo_block(kind, device[0]), sort_send.at[cut], sort_sem.at[kind], device
            )

    q_scale = math.log2(math.e) / HS**0.5

    def q_step(i, carry):
        rows = pl.ds(pl.multiple_of(i * group * blk, group * blk), group * blk)
        weight = wq[...].reshape(width, heads * HS)
        proj = jnp.dot(x[rows, :], weight, preferred_element_type=F32) * q_scale
        for r in range(group):
            for h in range(heads):
                piece = proj[r * blk : (r + 1) * blk, h * HS : (h + 1) * HS]
                q[i * group + r, h * blk : (h + 1) * blk, :] = piece.astype(BF16)
        return carry

    lax.fori_loop(0, slots // group, q_step, 0)

    token = lax.broadcasted_iota(jnp.int32, (blk, HS), 0)

    def masked(block, count):
        floats = block.astype(F32)
        live = token < count
        return (
            jnp.where(live, floats[:, :HS], 0.0).astype(BF16),
            jnp.where(live, floats[:, HS:], 0.0).astype(BF16),
            jnp.where(live, 1.0, 0.0).astype(BF16),
        )

    def near_step(s, carry):
        key, val, ones = masked(kv[s], lengths[first_node + s])
        near_v[s, :, :HS] = val
        near_v[s, :, HS:] = ones
        score = lax.dot_general(
            q[s], key, (((1,), (1,)), ((), ())), preferred_element_type=F32
        )
        row = lax.broadcasted_iota(jnp.int32, score.shape, 0) & (blk - 1)
        col = lax.broadcasted_iota(jnp.int32, score.shape, 1)
        near_w[s] = jnp.where(col <= row, jnp.exp2(score), 0.0).astype(BF16)
        return carry

    lax.fori_loop(0, slots, near_step, 0)
    stat[...] = jnp.zeros(stat.shape, F32)
    slice_copy.wait()
    g_kv.end()

    g_t.second_done()
    g_t.all_done()

    for cut, (device, _) in enumerate(sort_to):
        @pl.when(is_me(device))
        def _():
            sort_local[cut].wait()

    for kind in range(2):
        @pl.when(jnp.logical_not(is_me(sort_from[kind])))
        def _():
            await_recv(wo_block(kind, me), sort_send.at[0], sort_sem.at[kind], sort_from[kind])

    g_far.begin()

    def far_step(j, carry):
        node = parents[j, first_node]
        safe = jnp.maximum(node, 0)
        count = jnp.where(node >= 0, lengths[safe], 0)
        above = jnp.maximum(parents[jnp.maximum(j - 1, 0), first_node], 0)
        holder = jnp.where(j == 0, me, lax.div(above, slots))
        spot = table[lax.div(holder, 8), lax.div(lax.rem(holder, 8), 2), lax.rem(holder, 2)]
        key, val, ones = masked(spot, count)
        rows = pl.ds(pl.multiple_of(j * blk, blk), blk)
        keys[rows, :] = key
        vals[rows, :HS] = val
        vals[rows, HS:] = ones
        return carry

    lax.fori_loop(0, levels, far_step, 0)

    chunk = 512
    def attend(s):
        def score_step(j, carry):
            cols = pl.ds(pl.multiple_of(j * chunk, chunk), chunk)
            score = lax.dot_general(
                q[s], keys[cols, :], (((1,), (1,)), ((), ())), preferred_element_type=F32
            )
            far_w[:, cols] = jnp.exp2(score).astype(BF16)
            return carry

        lax.fori_loop(0, far // chunk, score_step, 0)
        both = jnp.dot(far_w[...], vals[...], preferred_element_type=F32)
        both = both + jnp.dot(near_w[s], near_v[s], preferred_element_type=F32)
        mean = both[:, :HS] * (1.0 / both[:, HS:]) * (1.0 / V_SCALE)
        for h in range(heads):
            attn[s, mp, :, h * HS : (h + 1) * HS] = mean[h * blk : (h + 1) * blk].astype(BF16)

    third = slots // 2

    def attn_sem_at(s, side, hop):
        return attn_sem.at[(s * 2 + side) * 3 + hop - 1]

    def attn_send(s, source, side, hop):
        ref = attn.at[s, source]
        start_copy(ref, ref, send_sem.at[0], attn_sem_at(s, side, hop), (plus, minus)[side])

    def relay(s, hop):
        j = halves[s // third][1]
        for side, left, more in ((0, j, j < 3), (1, 3 - j, j > 0)):
            source = mp_at(n_mp - hop if side == 0 else hop)

            @pl.when(left >= hop)
            def _():
                ref = attn.at[s, source]
                await_recv(ref, send_sem.at[0], attn_sem_at(s, side, hop), plus)

            if hop < 3:
                @pl.when((left >= hop) & more)
                def _():
                    attn_send(s, source, side, hop + 1)

    def attend_step(n, carry):
        cut = lax.rem(n, 2)
        s = cut * third + lax.div(n, 2)
        attend(s)
        _, j = place_of(mp, cut)

        @pl.when(j < 3)
        def _():
            attn_send(s, mp, 0, 1)

        @pl.when(j > 0)
        def _():
            attn_send(s, mp, 1, 1)

        @pl.when(n == 1)
        def _():
            g_far.first_done()
            g_own.begin()

        return carry

    lax.fori_loop(0, slots, attend_step, 0)

    def relays(u, hop):
        relay(u, hop)
        relay(third + u, hop)

    def product(s, cut, half, kind, first):
        rows = jnp.concatenate([attn[s, plane_at(cut, half, k)] for k in range(4)], axis=1)
        parts = []
        for pair in range(2):
            cols = []
            for r in (2 * pair, 2 * pair + 1):
                blocks = []
                for k in range(4):
                    t = k * 4 + r
                    blocks.append(wo[kind, first + t // 8, t % 8 // 2, t % 2])
                cols.append(jnp.concatenate(blocks, axis=0))
            weight = jnp.concatenate(cols, axis=1)
            parts.append(jnp.dot(rows, weight, preferred_element_type=F32))
        return jnp.concatenate(parts, axis=1)

    def across(u):
        s = end_cut * third + u
        for n in range(2):
            far_out[u, n] = product(s, end_cut, end_half, 1, 2 * n).astype(BF16)
            to = lax.rem(mp + outward * (n + 1), n_mp)
            start_copy(far_out.at[u, n], far_in.at[s], send_sem.at[2], cross_sem.at[s], (me, to))

    relays(0, 1)
    relays(1, 1)
    g_own.first_done()
    relays(0, 2)
    g_far.second_done()
    relays(2, 1)
    relays(1, 2)
    relays(0, 3)
    g_far.all_done()
    across(0)
    relays(2, 2)
    relays(1, 3)
    across(1)
    relays(2, 3)
    across(2)
    g_own.second_done()
    g_own.all_done()

    def own_step(u, carry):
        for cut in range(2):
            s = cut * third + u
            partial[s] = product(s, cut, halves[cut][0], 0, 2 * cut)
        return carry

    lax.fori_loop(0, third, own_step, 0)

    row = lax.broadcasted_iota(jnp.int32, (8, 128), 0)
    place = lax.broadcasted_iota(jnp.int32, (8, 128), 1)

    def hit_step(d, total):
        slot = jnp.int32(-1)
        for j in range(levels):
            spot = parents[j, d * slots] - first_node
            slot = jnp.where((spot >= 0) & (spot < slots), spot, slot)
        return total + jnp.where((row == slot) & (place == d), 1.0, 0.0)

    hits[...] = lax.fori_loop(0, n_dp, hit_step, jnp.zeros((8, 128), F32))

    g_q.end()
    g_far.end()
    g_own.end()
    g_t.end()
    route_end()
    for cut, (device, kind) in enumerate(sort_to):
        @pl.when(jnp.logical_not(is_me(device)))
        def _():
            await_send(w_out, sort_send.at[cut], sort_sem.at[0], device)

    def finish(s, carry):
        await_recv(far_in.at[s], send_sem.at[2], cross_sem.at[s], plus)
        total = partial[s] + far_in[s].astype(F32)
        result = (own_hidden[s].astype(F32) + total).astype(BF16)
        out[pl.ds(pl.multiple_of(s * blk, blk), blk), :] = result
        floats = result.astype(F32)
        heads_at = mp * (share // HS)
        head = jnp.concatenate(
            [w_head[pl.ds(heads_at + i, 1), :] for i in range(share // HS)], axis=1
        )
        weighted = floats * head
        floats = floats * floats
        for base, terms in ((0, floats), (8, weighted)):
            lanes = terms[:, :HS]
            for i in range(1, share // HS):
                lanes = lanes + terms[:, i * HS : (i + 1) * HS]
            stat[pl.ds(base + s, 1), :] = jnp.sum(lanes.T, axis=0, keepdims=True)
        return carry

    lax.fori_loop(0, slots, finish, 0)

    def stat_send(step, carry):
        start_copy(stat, stats.at[mp], send_sem.at[1], stat_sem.at[mp], (me, mp_at(step)))
        return carry

    def stat_wait(step, carry):
        source = mp_at(step)
        await_recv(stats.at[source], send_sem.at[1], stat_sem.at[source], (me, source))
        return carry

    lax.fori_loop(1, n_mp, stat_send, 0)
    stats[mp] = stat[...]
    lens = jnp.ones((8, 128), jnp.int32)
    for s in range(slots):
        lens = jnp.where(row == s, lengths[first_node + s], lens)
    lax.fori_loop(1, n_mp, stat_wait, 0)
    sums = jnp.sum(stats[...], axis=0)
    token_score = sums[8:] * lax.rsqrt(sums[:8] / width + 1e-05)
    node = jnp.sum(jnp.where(place < lens, token_score, 0.0), axis=1, keepdims=True)
    node = jnp.broadcast_to(node, token_score.shape) / lens.astype(F32)
    own = jnp.broadcast_to(jnp.sum(node, axis=0, keepdims=True), node.shape)
    tallies[0] = jnp.where(place == me, own, 0.0)

    def tally(level, sems, devices):
        for sem, device in zip(sems, devices):
            start_copy(
                tallies.at[level], tally_in.at[sem], tally_send.at[sem], tally_sem.at[sem],
                (device, mp),
            )
        total = tallies[level]
        for sem, device in zip(sems, devices):
            await_recv(tally_in.at[sem], tally_send.at[sem], tally_sem.at[sem], (device, mp))
            total = total + tally_in[sem]
        tallies[level + 1] = total

    tally(0, (0,), (g_kv.sibling,))
    tally(1, (1, 2, 3), [g_kv.device(step, 0) for step in (1, 2, 3)])
    tally(2, (4, 5, 6), [g_kv.device(0, step) for step in (1, 2, 3)])
    below = jnp.sum(hits[...] * tallies[3], axis=1, keepdims=True)
    values[...] = node + below
    await_send(attn.at[:, pl.ds(0, 3)], send_sem.at[0], attn_sem.at[0], plus)
    await_send(far_out, send_sem.at[2], cross_sem.at[0], plus)
    await_send(stats.at[pl.ds(0, n_mp - 1)], send_sem.at[1], stat_sem.at[0], plus)
    for sem in range(7):
        await_send(tallies.at[0], tally_send.at[sem], tally_sem.at[sem], plus)


def on_device(hidden, norm_gain, w_query, w_kv, w_out, w_head, parents, lengths):
    slots, blk, width = hidden.shape
    n_dp, n_mp = lax.axis_size("dp"), lax.axis_size("mp")
    levels = parents.shape[1]
    depth, q_columns = w_query.shape
    heads = q_columns // HS
    share = width // n_mp
    any_space = pl.BlockSpec(memory_space=pl.ANY)
    vmem = pl.BlockSpec(memory_space=pltpu.VMEM)
    smem = pl.BlockSpec(memory_space=pltpu.SMEM)
    dma = pltpu.SemaphoreType.DMA
    far = levels * blk
    layer, values = pl.pallas_call(
        functools.partial(kernel, n_dp, n_mp, slots, levels),
        out_shape=(
            jax.ShapeDtypeStruct((slots * blk, share), BF16),
            jax.ShapeDtypeStruct((8, 128), F32),
        ),
        in_specs=[any_space, vmem, any_space, any_space, any_space, vmem, smem, smem],
        out_specs=(vmem, vmem),
        scratch_shapes=[
            pltpu.VMEM((slots * blk, width), BF16),
            pltpu.VMEM((slots, blk, share), BF16),
            pltpu.VMEM((4, 4, 2, depth, q_columns), BF16),
            pltpu.VMEM((4, 4, 2, depth, 2 * HS), BF16),
            pltpu.VMEM((2, 4, 4, 2) + w_out.shape, BF16),
            pltpu.VMEM(w_kv.shape, BF16),
            pltpu.VMEM((1, width), F32),
            pltpu.VMEM((slots, heads * blk, HS), BF16),
            pltpu.VMEM((slots, blk, 2 * HS), BF16),
            pltpu.VMEM((4, 4, blk, 2 * HS), BF16),
            pltpu.VMEM((4, 4, blk, 2 * HS), BF16),
            pltpu.VMEM((3, 4, blk, 2 * HS), BF16),
            pltpu.VMEM((3, 4, blk, 2 * HS), BF16),
            pltpu.VMEM((4, blk, 2 * HS), BF16),
            pltpu.VMEM((3, blk, 2 * HS), BF16),
            pltpu.VMEM((3, blk, 2 * HS), BF16),
            pltpu.VMEM((4, 4, 2, blk, 2 * HS), BF16),
            pltpu.VMEM((far, HS), BF16),
            pltpu.VMEM((far, 2 * HS), BF16),
            pltpu.VMEM((slots, blk, 2 * HS), BF16),
            pltpu.VMEM((slots, heads * blk, blk), BF16),
            pltpu.VMEM((heads * blk, far), BF16),
            pltpu.VMEM((slots, n_mp, blk, q_columns), BF16),
            pltpu.VMEM((slots // 2, 2, blk, share), BF16),
            pltpu.VMEM((slots, blk, share), BF16),
            pltpu.VMEM((slots, blk, share), F32),
            pltpu.VMEM((16, 128), F32),
            pltpu.VMEM((n_mp, 16, 128), F32),
            pltpu.VMEM((4, 8, 128), F32),
            pltpu.VMEM((7, 8, 128), F32),
            pltpu.VMEM((8, 128), F32),
            dma((6 + slots,)),
            dma((10,)),
            dma((10,)),
            dma((10,)),
            dma((10,)),
            dma((10,)),
            dma((10,)),
            dma((10,)),
            dma((10,)),
            dma((10,)),
            dma((10,)),
            dma((2,)),
            dma((2,)),
            dma((10,)),
            dma((10,)),
            dma((3,)),
            dma((slots * 6,)),
            dma((slots,)),
            dma((n_mp,)),
            dma((7,)),
            dma((7,)),
        ],
        compiler_params=pltpu.CompilerParams(
            collective_id=0, has_side_effects=True, vmem_limit_bytes=60 * 1024 * 1024
        ),
    )(
        hidden, norm_gain.reshape(width // HS, HS), w_query, w_kv, w_out,
        w_head.reshape(width // HS, HS), parents.T, lengths,
    )
    return layer.reshape(slots, blk, share), values[:slots, 0]


def solution(mesh):
    in_specs = (
        P("dp", None, None),
        P(),
        P("dp", "mp"),
        P("dp", None, "mp"),
        P("mp", "dp"),
        P(),
        P(),
        P(),
    )
    out_specs = (P("dp", None, "mp"), P("dp"))
    return jax.shard_map(
        on_device, mesh=mesh, in_specs=in_specs, out_specs=out_specs, check_vma=False
    )
```

```python
import functools
import math

import jax
import jax.numpy as jnp
from jax import lax
from jax.experimental import pallas as pl
from jax.experimental.pallas import tpu as pltpu
from jax.sharding import PartitionSpec as P

HS = 128
V_SCALE = 2.0**-10
F32 = jnp.float32
BF16 = jnp.bfloat16
MESH = pl.DeviceIdType.MESH


def start_copy(src, dst, send_sem, recv_sem, device):
    pltpu.make_async_remote_copy(
        src_ref=src, dst_ref=dst, send_sem=send_sem, recv_sem=recv_sem,
        device_id=device, device_id_type=MESH,
    ).start()


def await_recv(ref, send_sem, recv_sem, device):
    pltpu.make_async_remote_copy(
        src_ref=ref, dst_ref=ref, send_sem=send_sem, recv_sem=recv_sem,
        device_id=device, device_id_type=MESH,
    ).wait_recv()


def await_send(ref, send_sem, recv_sem, device):
    pltpu.make_async_remote_copy(
        src_ref=ref, dst_ref=ref, send_sem=send_sem, recv_sem=recv_sem,
        device_id=device, device_id_type=MESH,
    ).wait_send()


class Gather:
    def __init__(self, whole, send_sems, sems, me, mp):
        self.whole, self.send_sems, self.sems = whole, send_sems, sems
        self.mp = mp
        self.core = lax.rem(me, 2)
        self.x = lax.rem(lax.div(me, 2), 4)
        self.y = lax.div(me, 8)
        self.sibling = me + 1 - 2 * self.core

    def device(self, first, second):
        on_x = jnp.where(self.core == 0, first, second)
        on_y = jnp.where(self.core == 0, second, first)
        return lax.rem(self.y + on_y, 4) * 8 + lax.rem(self.x + on_x, 4) * 2 + self.core

    def block(self, back):
        on_x = jnp.where(self.core == 0, 4 - back, 0)
        on_y = jnp.where(self.core == 0, 0, 4 - back)
        return self.whole.at[lax.rem(self.y + on_y, 4), lax.rem(self.x + on_x, 4), self.core]

    def line(self, core, back):
        if core == 0:
            return self.whole.at[lax.rem(self.y + 4 - back, 4), :, 0]
        return self.whole.at[:, lax.rem(self.x + 4 - back, 4), 1]

    def per_core(self, act):
        for core in range(2):
            @pl.when(self.core == core)
            def _():
                act(core)

    def copy(self, ref, sem, to):
        return pltpu.make_async_remote_copy(
            src_ref=ref, dst_ref=ref, send_sem=self.send_sems.at[sem],
            recv_sem=self.sems.at[sem], device_id=(to, self.mp), device_id_type=MESH,
        )

    def begin(self):
        for step in (1, 3, 2):
            self.copy(self.block(0), step - 1, self.device(step, 0)).start()

    def first_done(self):
        for step in (1, 3, 2):
            self.copy(self.block(step), step - 1, self.sibling).wait_recv()

        def act(core):
            for step in (1, 3, 2):
                self.copy(self.line(core, 0), 2 + step, self.device(0, step)).start()
            self.copy(self.line(core, 0), 6, self.sibling).start()

        self.per_core(act)

    def second_done(self):
        def act(core):
            for step in (1, 3, 2):
                self.copy(self.line(core, step), 2 + step, self.sibling).wait_recv()
                self.copy(self.line(core, step), 6 + step, self.sibling).start()

        self.per_core(act)

    def all_done(self):
        def act(core):
            for step in (0, 1, 3, 2):
                self.copy(self.line(1 - core, step), 6 + step, self.sibling).wait_recv()

        self.per_core(act)

    def end(self):
        def act(core):
            for step in range(3, 10):
                self.copy(self.line(core, 0), step, self.sibling).wait_send()

        for step in range(3):
            self.copy(self.block(0), step, self.sibling).wait_send()
        self.per_core(act)


def kernel(
    n_dp, n_mp, slots, levels,
    hidden, gain, w_query, w_kv, w_out, w_head, parents, lengths,
    out, values,
    x, own_hidden, wq, wkv, wo, kv_own, gains, q, kv, pair_out, pair_in, ring_out, ring_in, column_own,
    col_out, col_in, table, keys, vals, near_v, near_w, far_w,
    attn, far_out, far_in, partial, stat, stats, tallies, tally_in, hits,
    local_sem, kv_send, q_send, far_send, own_send, t_send, kv_sem, q_sem, far_sem, own_sem, t_sem, out_sem, sort_send,
    sort_sem, route_send, route_sem, send_sem, attn_sem, cross_sem, stat_sem, tally_send, tally_sem,
):
    me = lax.axis_index("dp")
    mp = lax.axis_index("mp")
    width = x.shape[1]
    blk = x.shape[0] // slots
    heads = wq.shape[-1] // HS
    share = out.shape[2]
    far = levels * blk
    core = lax.rem(me, 2)
    chip_x = lax.rem(lax.div(me, 2), 4)
    chip_y = lax.div(me, 8)
    first_node = me * slots

    def mp_at(step):
        return lax.rem(mp + step, n_mp)

    def place_of(plane, cut):
        i = lax.rem(plane + n_mp - 2 * cut, n_mp)
        return lax.div(i, 4), lax.rem(i, 4)

    def plane_at(cut, side, j):
        return lax.rem(2 * cut + side * 4 + j, n_mp)

    halves = [place_of(mp, cut) for cut in range(2)]
    end_cut = jnp.where((halves[0][1] == 0) | (halves[0][1] == 3), 0, 1)
    end_half, end_j = place_of(mp, end_cut)
    outward = jnp.where(end_j == 3, 1, n_mp - 1)

    def sort_target(cut):
        columns = lax.div(me, 4)
        their_half, their_j = place_of(columns, cut)
        half, j = place_of(mp, cut)
        same = their_half == half
        across = jnp.where(their_j < 2, their_j, 3 - their_j)
        end = plane_at(cut, half, jnp.where(their_j < 2, 3, 0))
        block = jnp.where(same, cut, across) * 16 + j * 4 + lax.rem(me, 4)
        return (block, jnp.where(same, columns, end)), jnp.where(same, 0, 1)

    def sort_source(kind):
        which, j, column = lax.div(me, 16), lax.div(lax.rem(me, 16), 4), lax.rem(me, 4)
        if kind == 0:
            half = jnp.where(which == 0, halves[0][0], halves[1][0])
            return mp * 4 + column, plane_at(which, half, j)
        columns = lax.rem(mp + outward * (which + 1), n_mp)
        return columns * 4 + column, plane_at(end_cut, end_half, j)

    def is_me(device):
        return (device[0] == me) & (device[1] == mp)

    sort_to = [sort_target(cut) for cut in range(2)]
    sort_from = [sort_source(kind) for kind in range(2)]
    strangers = [device for device, _ in sort_to] + sort_from

    def wo_block(kind, block):
        return wo.at[kind, lax.div(block, 8), lax.div(lax.rem(block, 8), 2), lax.rem(block, 2)]

    kv_copy = pltpu.make_async_copy(w_kv, kv_own, local_sem.at[0])
    q_copy = pltpu.make_async_copy(w_query, wq.at[chip_y, chip_x, core], local_sem.at[1])
    hidden_copies = [
        pltpu.make_async_copy(hidden.at[s], x.at[pl.ds(s * blk, blk), :], local_sem.at[4 + s])
        for s in range(slots)
    ]
    column = pl.multiple_of(mp * share, share)
    slice_copy = pltpu.make_async_copy(
        hidden.at[:, :, pl.ds(column, share)], own_hidden, local_sem.at[3]
    )
    kv_copy.start()
    for copy in hidden_copies:
        copy.start()
    q_copy.start()
    slice_copy.start()

    barrier = pltpu.get_barrier_semaphore()

    def greet(device):
        pl.semaphore_signal(barrier, inc=1, device_id=device, device_id_type=MESH)

    def greet_mp(step, carry):
        greet((me, mp_at(step)))
        return carry

    g_kv = Gather(wkv, kv_send, kv_sem, me, mp)
    g_q = Gather(wq, q_send, q_sem, me, mp)
    g_far = Gather(wo.at[1], far_send, far_sem, me, mp)
    g_own = Gather(wo.at[0], own_send, own_sem, me, mp)
    g_t = Gather(table, t_send, t_sem, me, mp)
    def dp_near(on_x, on_y, flip):
        chip = lax.rem(chip_y + on_y, 4) * 8 + lax.rem(chip_x + on_x, 4) * 2
        return chip + lax.rem(core + flip, 2)

    row_devices = [dp_near(i, 0, flip) for flip in (0, 1) for i in (2, 1, 3)] + [dp_near(0, 0, 1)]
    column_devices = [dp_near(0, i, 0) for i in (2, 1, 3)]
    for device in row_devices + column_devices:
        greet((device, mp))
    lax.fori_loop(1, n_mp, greet_mp, 0)

    for stranger in strangers:
        @pl.when(jnp.logical_not(is_me(stranger)))
        def _():
            greet(stranger)

    for i in range(width // HS):
        gains[:, i * HS : (i + 1) * HS] = gain[i : i + 1, :].astype(F32)

    def norm_segment(s):
        hidden_copies[s].wait()

        def rows_step(r, carry):
            rows = pl.ds(pl.multiple_of(s * blk + r * 16, 16), 16)
            floats = x[rows, :].astype(F32)
            meansq = jnp.mean(floats * floats, axis=-1, keepdims=True)
            scaled = floats * lax.rsqrt(meansq + 1e-05)
            x[rows, :] = (scaled * gains[...]).astype(BF16)
            return carry

        lax.fori_loop(0, blk // 16, rows_step, 0)

    kv_copy.wait()
    wkv[chip_y, chip_x, core, :, :HS] = kv_own[:, 0, :]
    wkv[chip_y, chip_x, core, :, HS:] = kv_own[:, 1, :]
    norm_segment(0)
    norm_segment(1)
    peers = 10 + n_mp - 1
    for stranger in strangers:
        peers = peers + jnp.where(is_me(stranger), 0, 1)
    pl.semaphore_wait(barrier, peers)

    g_kv.begin()
    q_copy.wait()
    g_q.begin()
    norm_segment(2)
    norm_segment(3)
    g_kv.first_done()
    norm_segment(4)
    norm_segment(5)
    g_q.first_done()
    g_kv.second_done()
    g_kv.all_done()

    group = slots // 2

    def kv_step(i, carry):
        rows = pl.ds(pl.multiple_of(i * group * blk, group * blk), group * blk)
        weight = wkv[...].reshape(width, 2 * HS)
        proj = jnp.dot(x[rows, :], weight, preferred_element_type=F32)
        for r in range(group):
            piece = proj[r * blk : (r + 1) * blk]
            kv[i * group + r, :, :HS] = piece[:, :HS].astype(BF16)
            kv[i * group + r, :, HS:] = (piece[:, HS:] * V_SCALE).astype(BF16)
        return carry

    lax.fori_loop(0, slots // group, kv_step, 0)

    f0 = jnp.where(core == 0, chip_x, chip_y)
    g0 = jnp.where(core == 0, chip_y, chip_x)
    f_mul = jnp.where(core == 0, 2, 8)
    g_mul = jnp.where(core == 0, 8, 2)

    def wanted(device):
        place = parents[0, device * slots] - first_node
        found = (place >= 0) & (place < slots)
        block = kv[jnp.clip(place, 0, slots - 1)]
        return jnp.where(found, block, jnp.zeros_like(block))

    def at4(value):
        return lax.rem(value, 4)

    for step in (2, 1, 3, 0):
        line = at4(g0 + step)
        for k in range(4):
            pair_out[step, k] = wanted(line * g_mul + k * f_mul + 1 - core)
        start_copy(
            pair_out.at[step], pair_in.at[step], route_send.at[step], route_sem.at[step],
            (g_kv.sibling, mp),
        )
    for step in (2, 1, 3, 0):
        await_recv(pair_in.at[step], route_send.at[step], route_sem.at[step], (g_kv.sibling, mp))
        line = at4(f0 + step)
        target = column_own if step == 0 else ring_out.at[step - 1]
        for k in range(4):
            target[k] = wanted(line * f_mul + k * g_mul + core) + pair_in[step, k]
        if step > 0:
            start_copy(
                ring_out.at[step - 1], ring_in.at[step - 1], route_send.at[3 + step],
                route_sem.at[3 + step], (g_kv.device(step, 0), mp),
            )

    def route_ring():
        for step in (1, 3, 2):
            await_recv(
                ring_in.at[step - 1], route_send.at[3 + step], route_sem.at[3 + step],
                (g_kv.sibling, mp),
            )

        def total(k):
            return column_own[k] + ring_in[0, k] + ring_in[1, k] + ring_in[2, k]

        for step in (2, 1, 3):
            col_out[step - 1] = total(at4(g0 + step))
            start_copy(
                col_out.at[step - 1], col_in.at[step - 1], route_send.at[6 + step],
                route_sem.at[6 + step], (g_kv.device(0, step), mp),
            )
        table[chip_y, chip_x, core] = total(g0)

    def route_column():
        for step in (1, 3, 2):
            await_recv(
                col_in.at[step - 1], route_send.at[6 + step], route_sem.at[6 + step],
                (g_kv.sibling, mp),
            )
        mine = table[chip_y, chip_x, core] + col_in[0] + col_in[1] + col_in[2]
        table[chip_y, chip_x, core] = mine
        g_t.begin()

    def route_end():
        for step in range(4):
            await_send(pair_out.at[step], route_send.at[step], route_sem.at[step], plus)
        for step in range(3):
            await_send(ring_out.at[step], route_send.at[4 + step], route_sem.at[4 + step], plus)
            await_send(col_out.at[step], route_send.at[7 + step], route_sem.at[7 + step], plus)

    plus, minus = (me, mp_at(1)), (me, mp_at(n_mp - 1))

    route_ring()
    route_column()
    g_q.second_done()
    g_t.first_done()
    g_q.all_done()

    sort_local = [
        pltpu.make_async_copy(w_out, wo_block(kind, device[0]), local_sem.at[4 + slots + cut])
        for cut, (device, kind) in enumerate(sort_to)
    ]
    for cut, (device, kind) in enumerate(sort_to):
        @pl.when(is_me(device))
        def _():
            sort_local[cut].start()

        @pl.when(jnp.logical_not(is_me(device)))
        def _():
            start_copy(
                w_out, wo_block(kind, device[0]), sort_send.at[cut], sort_sem.at[kind], device
            )

    q_scale = math.log2(math.e) / HS**0.5

    def q_step(i, carry):
        rows = pl.ds(pl.multiple_of(i * group * blk, group * blk), group * blk)
        weight = wq[...].reshape(width, heads * HS)
        proj = jnp.dot(x[rows, :], weight, preferred_element_type=F32) * q_scale
        for r in range(group):
            for h in range(heads):
                piece = proj[r * blk : (r + 1) * blk, h * HS : (h + 1) * HS]
                q[i * group + r, h * blk : (h + 1) * blk, :] = piece.astype(BF16)
        return carry

    lax.fori_loop(0, slots // group, q_step, 0)

    token = lax.broadcasted_iota(jnp.int32, (blk, HS), 0)

    def masked(block, count):
        floats = block.astype(F32)
        live = token < count
        return (
            jnp.where(live, floats[:, :HS], 0.0).astype(BF16),
            jnp.where(live, floats[:, HS:], 0.0).astype(BF16),
            jnp.where(live, 1.0, 0.0).astype(BF16),
        )

    def near_step(s, carry):
        key, val, ones = masked(kv[s], lengths[first_node + s])
        near_v[s, :, :HS] = val
        near_v[s, :, HS:] = ones
        score = lax.dot_general(
            q[s], key, (((1,), (1,)), ((), ())), preferred_element_type=F32
        )
        row = lax.broadcasted_iota(jnp.int32, score.shape, 0) & (blk - 1)
        col = lax.broadcasted_iota(jnp.int32, score.shape, 1)
        near_w[s] = jnp.where(col <= row, jnp.exp2(score), 0.0).astype(BF16)
        return carry

    lax.fori_loop(0, slots, near_step, 0)
    stat[...] = jnp.zeros(stat.shape, F32)
    slice_copy.wait()
    g_kv.end()

    g_t.second_done()
    g_t.all_done()

    for cut, (device, _) in enumerate(sort_to):
        @pl.when(is_me(device))
        def _():
            sort_local[cut].wait()

    for kind in range(2):
        @pl.when(jnp.logical_not(is_me(sort_from[kind])))
        def _():
            await_recv(wo_block(kind, me), sort_send.at[0], sort_sem.at[kind], sort_from[kind])

    g_far.begin()

    def far_step(j, carry):
        node = parents[j, first_node]
        safe = jnp.maximum(node, 0)
        count = jnp.where(node >= 0, lengths[safe], 0)
        above = jnp.maximum(parents[jnp.maximum(j - 1, 0), first_node], 0)
        holder = jnp.where(j == 0, me, lax.div(above, slots))
        spot = table[lax.div(holder, 8), lax.div(lax.rem(holder, 8), 2), lax.rem(holder, 2)]
        key, val, ones = masked(spot, count)
        rows = pl.ds(pl.multiple_of(j * blk, blk), blk)
        keys[rows, :] = key
        vals[rows, :HS] = val
        vals[rows, HS:] = ones
        return carry

    lax.fori_loop(0, levels, far_step, 0)

    chunk = 512
    def attend(s):
        def score_step(j, carry):
            cols = pl.ds(pl.multiple_of(j * chunk, chunk), chunk)
            score = lax.dot_general(
                q[s], keys[cols, :], (((1,), (1,)), ((), ())), preferred_element_type=F32
            )
            far_w[:, cols] = jnp.exp2(score).astype(BF16)
            return carry

        lax.fori_loop(0, far // chunk, score_step, 0)
        both = jnp.dot(far_w[...], vals[...], preferred_element_type=F32)
        both = both + jnp.dot(near_w[s], near_v[s], preferred_element_type=F32)
        mean = both[:, :HS] * (1.0 / both[:, HS:]) * (1.0 / V_SCALE)
        for h in range(heads):
            attn[s, mp, :, h * HS : (h + 1) * HS] = mean[h * blk : (h + 1) * blk].astype(BF16)

    third = slots // 2

    def attn_sem_at(s, side, hop):
        return attn_sem.at[(s * 2 + side) * 3 + hop - 1]

    def attn_send(s, source, side, hop):
        ref = attn.at[s, source]
        start_copy(ref, ref, send_sem.at[0], attn_sem_at(s, side, hop), (plus, minus)[side])

    def relay(s, hop):
        j = halves[s // third][1]
        for side, left, more in ((0, j, j < 3), (1, 3 - j, j > 0)):
            source = mp_at(n_mp - hop if side == 0 else hop)

            @pl.when(left >= hop)
            def _():
                ref = attn.at[s, source]
                await_recv(ref, send_sem.at[0], attn_sem_at(s, side, hop), plus)

            if hop < 3:
                @pl.when((left >= hop) & more)
                def _():
                    attn_send(s, source, side, hop + 1)

    def attend_step(n, carry):
        cut = lax.rem(n, 2)
        s = cut * third + lax.div(n, 2)
        attend(s)
        _, j = place_of(mp, cut)

        @pl.when(j < 3)
        def _():
            attn_send(s, mp, 0, 1)

        @pl.when(j > 0)
        def _():
            attn_send(s, mp, 1, 1)

        @pl.when(n == 1)
        def _():
            g_far.first_done()
            g_own.begin()

        return carry

    lax.fori_loop(0, slots, attend_step, 0)

    def relays(u, hop):
        relay(u, hop)
        relay(third + u, hop)

    def product(s, cut, half, kind, first):
        rows = jnp.concatenate([attn[s, plane_at(cut, half, k)] for k in range(4)], axis=1)
        parts = []
        for pair in range(2):
            cols = []
            for r in (2 * pair, 2 * pair + 1):
                blocks = []
                for k in range(4):
                    t = k * 4 + r
                    blocks.append(wo[kind, first + t // 8, t % 8 // 2, t % 2])
                cols.append(jnp.concatenate(blocks, axis=0))
            weight = jnp.concatenate(cols, axis=1)
            parts.append(jnp.dot(rows, weight, preferred_element_type=F32))
        return jnp.concatenate(parts, axis=1)

    def across(u):
        s = end_cut * third + u
        for n in range(2):
            far_out[u, n] = product(s, end_cut, end_half, 1, 2 * n).astype(BF16)
            to = lax.rem(mp + outward * (n + 1), n_mp)
            start_copy(far_out.at[u, n], far_in.at[s], send_sem.at[2], cross_sem.at[s], (me, to))

    relays(0, 1)
    g_own.first_done()
    relays(0, 2)
    relays(1, 1)
    relays(0, 3)
    relays(1, 2)
    relays(2, 1)
    g_far.second_done()
    g_far.all_done()
    across(0)
    relays(1, 3)
    relays(2, 2)
    across(1)
    relays(2, 3)
    across(2)
    g_own.second_done()
    g_own.all_done()

    def own_step(u, carry):
        for cut in range(2):
            s = cut * third + u
            partial[s] = product(s, cut, halves[cut][0], 0, 2 * cut)
        return carry

    lax.fori_loop(0, third, own_step, 0)

    row = lax.broadcasted_iota(jnp.int32, (8, 128), 0)
    place = lax.broadcasted_iota(jnp.int32, (8, 128), 1)

    def hit_step(d, total):
        slot = jnp.int32(-1)
        for j in range(levels):
            spot = parents[j, d * slots] - first_node
            slot = jnp.where((spot >= 0) & (spot < slots), spot, slot)
        return total + jnp.where((row == slot) & (place == d), 1.0, 0.0)

    hits[...] = lax.fori_loop(0, n_dp, hit_step, jnp.zeros((8, 128), F32))

    g_q.end()
    g_far.end()
    g_own.end()
    g_t.end()
    route_end()
    for cut, (device, kind) in enumerate(sort_to):
        @pl.when(jnp.logical_not(is_me(device)))
        def _():
            await_send(w_out, sort_send.at[cut], sort_sem.at[0], device)

    def out_copy(s):
        return pltpu.make_async_copy(own_hidden.at[s], out.at[s], out_sem.at[s])

    def finish(n, carry):
        s = lax.rem(n, 2) * third + lax.div(n, 2)
        await_recv(far_in.at[s], send_sem.at[2], cross_sem.at[s], plus)
        total = partial[s] + far_in[s].astype(F32)
        result = (own_hidden[s].astype(F32) + total).astype(BF16)
        own_hidden[s] = result
        out_copy(s).start()
        floats = result.astype(F32)
        heads_at = mp * (share // HS)
        head = jnp.concatenate(
            [w_head[pl.ds(heads_at + i, 1), :] for i in range(share // HS)], axis=1
        )
        weighted = floats * head
        floats = floats * floats
        for base, terms in ((0, floats), (8, weighted)):
            lanes = terms[:, :HS]
            for i in range(1, share // HS):
                lanes = lanes + terms[:, i * HS : (i + 1) * HS]
            stat[pl.ds(base + s, 1), :] = jnp.sum(lanes.T, axis=0, keepdims=True)
        return carry

    lax.fori_loop(0, slots, finish, 0)

    def stat_send(step, carry):
        start_copy(stat, stats.at[mp], send_sem.at[1], stat_sem.at[mp], (me, mp_at(step)))
        return carry

    def stat_wait(step, carry):
        source = mp_at(step)
        await_recv(stats.at[source], send_sem.at[1], stat_sem.at[source], (me, source))
        return carry

    lax.fori_loop(1, n_mp, stat_send, 0)
    stats[mp] = stat[...]
    lens = jnp.ones((8, 128), jnp.int32)
    for s in range(slots):
        lens = jnp.where(row == s, lengths[first_node + s], lens)
    lax.fori_loop(1, n_mp, stat_wait, 0)
    sums = jnp.sum(stats[...], axis=0)
    token_score = sums[8:] * lax.rsqrt(sums[:8] / width + 1e-05)
    node = jnp.sum(jnp.where(place < lens, token_score, 0.0), axis=1, keepdims=True)
    node = jnp.broadcast_to(node, token_score.shape) / lens.astype(F32)
    own = jnp.broadcast_to(jnp.sum(node, axis=0, keepdims=True), node.shape)
    tallies[0] = jnp.where(place == me, own, 0.0)

    def tally(level, sems, devices):
        for sem, device in zip(sems, devices):
            start_copy(
                tallies.at[level], tally_in.at[sem], tally_send.at[sem], tally_sem.at[sem],
                (device, mp),
            )
        total = tallies[level]
        for sem, device in zip(sems, devices):
            await_recv(tally_in.at[sem], tally_send.at[sem], tally_sem.at[sem], (device, mp))
            total = total + tally_in[sem]
        tallies[level + 1] = total

    tally(0, range(7), row_devices)
    tally(1, range(7, 10), column_devices)
    below = jnp.sum(hits[...] * tallies[2], axis=1, keepdims=True)
    values[...] = node + below
    await_send(attn.at[:, pl.ds(0, 3)], send_sem.at[0], attn_sem.at[0], plus)
    await_send(far_out, send_sem.at[2], cross_sem.at[0], plus)
    await_send(stats.at[pl.ds(0, n_mp - 1)], send_sem.at[1], stat_sem.at[0], plus)
    for s in range(slots):
        out_copy(s).wait()
    for sem in range(10):
        await_send(tallies.at[0], tally_send.at[sem], tally_sem.at[sem], plus)


def on_device(hidden, norm_gain, w_query, w_kv, w_out, w_head, parents, lengths):
    slots, blk, width = hidden.shape
    n_dp, n_mp = lax.axis_size("dp"), lax.axis_size("mp")
    levels = parents.shape[1]
    depth, q_columns = w_query.shape
    heads = q_columns // HS
    share = width // n_mp
    any_space = pl.BlockSpec(memory_space=pl.ANY)
    vmem = pl.BlockSpec(memory_space=pltpu.VMEM)
    smem = pl.BlockSpec(memory_space=pltpu.SMEM)
    dma = pltpu.SemaphoreType.DMA
    far = levels * blk
    layer, values = pl.pallas_call(
        functools.partial(kernel, n_dp, n_mp, slots, levels),
        out_shape=(
            jax.ShapeDtypeStruct((slots, blk, share), BF16),
            jax.ShapeDtypeStruct((8, 128), F32),
        ),
        in_specs=[any_space, vmem, any_space, any_space, any_space, vmem, smem, smem],
        out_specs=(any_space, vmem),
        scratch_shapes=[
            pltpu.VMEM((slots * blk, width), BF16),
            pltpu.VMEM((slots, blk, share), BF16),
            pltpu.VMEM((4, 4, 2, depth, q_columns), BF16),
            pltpu.VMEM((4, 4, 2, depth, 2 * HS), BF16),
            pltpu.VMEM((2, 4, 4, 2) + w_out.shape, BF16),
            pltpu.VMEM(w_kv.shape, BF16),
            pltpu.VMEM((1, width), F32),
            pltpu.VMEM((slots, heads * blk, HS), BF16),
            pltpu.VMEM((slots, blk, 2 * HS), BF16),
            pltpu.VMEM((4, 4, blk, 2 * HS), BF16),
            pltpu.VMEM((4, 4, blk, 2 * HS), BF16),
            pltpu.VMEM((3, 4, blk, 2 * HS), BF16),
            pltpu.VMEM((3, 4, blk, 2 * HS), BF16),
            pltpu.VMEM((4, blk, 2 * HS), BF16),
            pltpu.VMEM((3, blk, 2 * HS), BF16),
            pltpu.VMEM((3, blk, 2 * HS), BF16),
            pltpu.VMEM((4, 4, 2, blk, 2 * HS), BF16),
            pltpu.VMEM((far, HS), BF16),
            pltpu.VMEM((far, 2 * HS), BF16),
            pltpu.VMEM((slots, blk, 2 * HS), BF16),
            pltpu.VMEM((slots, heads * blk, blk), BF16),
            pltpu.VMEM((heads * blk, far), BF16),
            pltpu.VMEM((slots, n_mp, blk, q_columns), BF16),
            pltpu.VMEM((slots // 2, 2, blk, share), BF16),
            pltpu.VMEM((slots, blk, share), BF16),
            pltpu.VMEM((slots, blk, share), F32),
            pltpu.VMEM((16, 128), F32),
            pltpu.VMEM((n_mp, 16, 128), F32),
            pltpu.VMEM((3, 8, 128), F32),
            pltpu.VMEM((10, 8, 128), F32),
            pltpu.VMEM((8, 128), F32),
            dma((6 + slots,)),
            dma((10,)),
            dma((10,)),
            dma((10,)),
            dma((10,)),
            dma((10,)),
            dma((10,)),
            dma((10,)),
            dma((10,)),
            dma((10,)),
            dma((10,)),
            dma((slots,)),
            dma((2,)),
            dma((2,)),
            dma((10,)),
            dma((10,)),
            dma((3,)),
            dma((slots * 6,)),
            dma((slots,)),
            dma((n_mp,)),
            dma((10,)),
            dma((10,)),
        ],
        compiler_params=pltpu.CompilerParams(
            collective_id=0, has_side_effects=True, vmem_limit_bytes=60 * 1024 * 1024
        ),
    )(
        hidden, norm_gain.reshape(width // HS, HS), w_query, w_kv, w_out,
        w_head.reshape(width // HS, HS), parents.T, lengths,
    )
    return layer, values[:slots, 0]


def solution(mesh):
    in_specs = (
        P("dp", None, None),
        P(),
        P("dp", "mp"),
        P("dp", None, "mp"),
        P("mp", "dp"),
        P(),
        P(),
        P(),
    )
    out_specs = (P("dp", None, "mp"), P("dp"))
    return jax.shard_map(
        on_device, mesh=mesh, in_specs=in_specs, out_specs=out_specs, check_vma=False
    )
```
